512 devices in a mesh: slide: 8 (over y_lo, x), seq: 64 (over z, y_hi, core).
Axes of the slice: x: 4, y: 4 (y_hi: 2, y_lo: 2; y = y_hi * 2 + y_lo), z: 16, core: 2. Of those that a mesh axis runs over, the one named last changes fastest.
Arguments:
- tokens: bfloat16 [8, 8192, 768], P('slide', 'seq'), may hold values from -12 to 12
- lengths: int32 [8], P('slide'), may hold values from 2048 to 8192, as said below
- w_query: bfloat16 [768, 384], P('seq'), may hold values from -0.21875 to 0.21875
- w_key: bfloat16 [768, 384], P('seq'), may hold values from -0.21875 to 0.21875
- w_value: bfloat16 [768, 384], P('seq'), may hold values from -0.21875 to 0.21875
- w_out: bfloat16 [384, 768], P('seq'), may hold values from -0.3125 to 0.3125
- grad_out: bfloat16 [8, 8192, 768], P('slide', 'seq'), may hold values from -6 to 6
Outputs:
- mixed: bfloat16 [8, 8192, 768], P('slide', 'seq')
- grad_tokens: bfloat16 [8, 8192, 768], P('slide', 'seq')
- grad_value_weight: float32 [768, 384], P('seq')
- grad_out_weight: float32 [384, 768], P('seq')
The draws below stay inside these ranges and needn't reach their ends.
Inputs may be any that keep to these rules, and one draw needn't show every extreme that they name: `lengths`: each slide's count of valid tile tokens lies between 2048 and 8192, and some slide is full.
All inputs are finite; a program needn't handle non-finite values.
Results may differ from the reference program's by a relative error of at most 0.013.
The reference program's roundings to bfloat16 on the way (of `weights`, `attended`, `grad_attended` and `grad_scores`) count: a program that leaves them out, or rounds other values in their place, can miss the bound.
Values may be sent and summed in bfloat16 or wider, within the bound.
No kernel may reach another device: no remote copies, remote signals or barrier semaphores. Data moves between devices by JAX's collectives and lax.ppermute only.
A program may use at most 64 MiB of HBM per device.

```python
import jax
import jax.numpy as jnp
from jax import lax

D = 768
HEADS = 8
SCALES = 5
TOK_DEV = 128
INNER = 384
SEQ = 8192
SLIDES = 8


def draw_tokens(key, part):
    key = jax.random.fold_in(key, 11)
    shape = (SLIDES, SEQ, D)
    key_base = jax.random.fold_in(key, 0)
    values = jax.random.normal(key_base, shape, jnp.float32)
    return jnp.clip(values, -12.0, 12.0).astype(jnp.bfloat16)


def draw_lengths(key, part):
    key = jax.random.fold_in(key, 23)
    key_len, key_full = jax.random.split(key)
    values = jax.random.randint(key_len, (SLIDES,), SEQ // 4, SEQ + 1, dtype=jnp.int32)
    full_slide = jax.random.randint(key_full, (), 0, SLIDES, dtype=jnp.int32)
    slide_index = jnp.arange(SLIDES, dtype=jnp.int32)
    return jnp.where(slide_index == full_slide, jnp.int32(SEQ), values)


def shard_levels(key, extent, cuts, low, largest):
    def one(dim, blocks):
        draws = jax.random.uniform(jax.random.fold_in(jax.random.fold_in(key, 6), dim), (blocks,), jnp.float32, low / len(cuts), largest / len(cuts))
        return jnp.repeat(jnp.exp(draws), extent[dim] // blocks).reshape((-1,) + (1,) * (len(extent) - dim - 1))

    gain = one(*cuts[0])
    for cut in cuts[1:]:
        gain = gain * one(*cut)
    return gain


def normal_values(own_key, shape, deviation, bound, cuts=(), kind=jnp.bfloat16):
    values = jax.random.normal(own_key, shape, jnp.float32) * deviation
    if len(cuts) > 0:
        values = shard_levels(own_key, shape, cuts, -0.22, 0.18) * values
    return jnp.clip(values, min=-bound, max=bound).astype(kind)


def setup_inputs(seed: int = 0) -> dict:
    seeds = jax.random.split(jax.random.key(seed), 8)
    return {
        "tokens": draw_tokens(jax.random.fold_in(seeds[7], 71), 0),
        "lengths": draw_lengths(jax.random.fold_in(seeds[7], 71), 0),
        "w_query": normal_values(seeds[2], (D, INNER), D ** -0.5, 0.21875, ((0, 64),)),
        "w_key": normal_values(seeds[3], (D, INNER), D ** -0.5, 0.21875, ((0, 64),)),
        "w_value": normal_values(seeds[4], (D, INNER), D ** -0.5, 0.21875, ((0, 64),)),
        "w_out": normal_values(seeds[5], (INNER, D), INNER ** -0.5, 0.3125, ((0, 64),)),
        "grad_out": normal_values(seeds[6], (SLIDES, SEQ, D), 1.0, 6.0, ((0, 8), (1, 64))),
    }


def dilate(rows, rate, head_count):
    count = rows.shape[0] // rate
    shaped = rows.reshape(count, rate, 2, head_count, -1)
    pick = (jnp.arange(rate, dtype=jnp.int32)[:, None] == (jnp.arange(head_count, dtype=jnp.int32) % rate)[None, :]).astype(rows.dtype)
    return jnp.sum(shaped * pick[None, :, None, :, None], axis=1).reshape(count, 2, -1)


def spread(rows, rate, head_count):
    count = rows.shape[0]
    pick = (jnp.arange(rate, dtype=jnp.int32)[:, None] == (jnp.arange(head_count, dtype=jnp.int32) % rate)[None, :]).astype(rows.dtype)
    shaped = rows.reshape(count, 1, 2, head_count, -1) * pick[None, :, None, :, None]
    return shaped.reshape(count * rate, 2, -1)


def block_masks(block, length, tok, head_count):
    heads_index = jnp.arange(head_count, dtype=jnp.int32)
    rows_index = jnp.arange(tok, dtype=jnp.int32)
    masks = []
    for scale in range(SCALES):
        rate = 2 ** scale
        count = tok // rate
        start = (block // rate) * rate
        member = rows_index // count
        within = rows_index % count
        position = (start + member)[None, :] * tok + within[None, :] * rate + (heads_index % rate)[:, None]
        key_valid = position < length
        query_part = (rows_index[None, :] % rate) == (heads_index[:, None] % rate)
        masks.append(query_part[:, :, None] & key_valid[:, None, :])
    return jnp.concatenate(masks, axis=2)


def probabilities(query, keys, allowed):
    scale_factor = query.shape[1] ** -0.5
    scores = lax.dot_general(query, keys, (((1,), (1,)), ((), ())), preferred_element_type=jnp.float32) * scale_factor
    scores = jnp.where(allowed, scores, jnp.float32(-1e9))
    top = jnp.max(scores, axis=1, keepdims=True)
    expo = jnp.exp(scores - top)
    return expo / jnp.sum(expo, axis=1, keepdims=True)


def forward_head(query, keys, values, allowed):
    probs = probabilities(query, keys, allowed)
    return jnp.dot(probs.astype(jnp.bfloat16), values, preferred_element_type=jnp.float32)


def backward_head(query, keys, values, allowed, upstream):
    scale_factor = query.shape[1] ** -0.5
    probs = probabilities(query, keys, allowed)
    weights = probs.astype(jnp.bfloat16)
    grad_probs = lax.dot_general(upstream, values, (((1,), (1,)), ((), ())), preferred_element_type=jnp.float32)
    delta = jnp.sum(probs * grad_probs, axis=1, keepdims=True)
    grad_scores = (probs * (grad_probs - delta)).astype(jnp.bfloat16)
    grad_query = jnp.dot(grad_scores, keys, preferred_element_type=jnp.float32) * scale_factor
    grad_key = lax.dot_general(grad_scores, query, (((0,), (0,)), ((), ())), preferred_element_type=jnp.float32) * scale_factor
    grad_value = lax.dot_general(weights, upstream, (((0,), (0,)), ((), ())), preferred_element_type=jnp.float32)
    return grad_query, grad_key, grad_value


def split_heads(rows, head_count):
    return rows.reshape(rows.shape[0], head_count, -1).transpose(1, 0, 2)


def reference(tokens, lengths, w_query, w_key, w_value, w_out, grad_out):
    tok = TOK_DEV
    head_count = HEADS
    inner = INNER
    count_blocks = SEQ // tok
    block_ids = jnp.arange(count_blocks, dtype=jnp.int32)
    grad_value_weight = jnp.zeros((D, inner), jnp.float32)
    grad_out_weight = jnp.zeros((inner, D), jnp.float32)
    mixed_list = []
    grad_list = []
    for slide in range(SLIDES):
        inputs = tokens[slide]
        upstream = grad_out[slide]
        length = lengths[slide]
        query = jnp.dot(inputs, w_query, preferred_element_type=jnp.float32).astype(jnp.bfloat16)
        pairs = jnp.stack([jnp.dot(inputs, w_key, preferred_element_type=jnp.float32).astype(jnp.bfloat16),
                           jnp.dot(inputs, w_value, preferred_element_type=jnp.float32).astype(jnp.bfloat16)], axis=1)

        def gather_block(block):
            pieces = []
            for scale in range(SCALES):
                rate = 2 ** scale
                start = (block // rate) * rate * tok
                segment = lax.dynamic_slice_in_dim(pairs, start, rate * tok, 0)
                pieces.append(dilate(segment, rate, head_count))
            keys = jnp.concatenate(pieces, axis=0)
            query_block = lax.dynamic_slice_in_dim(query, block * tok, tok, 0)
            return (split_heads(query_block, head_count), split_heads(keys[:, 0], head_count),
                    split_heads(keys[:, 1], head_count), block_masks(block, length, tok, head_count))

        def forward_block(block):
            query_heads, key_heads, value_heads, allowed = gather_block(block)
            outputs = lax.map(lambda item: forward_head(*item), (query_heads, key_heads, value_heads, allowed))
            return outputs.transpose(1, 0, 2).reshape(tok, inner)

        outputs = lax.map(forward_block, block_ids).reshape(SEQ, inner)
        valid = (jnp.arange(SEQ, dtype=jnp.int32) < length)[:, None]
        attended = jnp.where(valid, outputs, jnp.float32(0.0)).astype(jnp.bfloat16)
        mixed_list.append(jnp.dot(attended, w_out, preferred_element_type=jnp.float32).astype(jnp.bfloat16))
        grad_out_weight = grad_out_weight + lax.dot_general(attended, upstream, (((0,), (0,)), ((), ())), preferred_element_type=jnp.float32)
        grad_attended = lax.dot_general(upstream, w_out, (((1,), (1,)), ((), ())), preferred_element_type=jnp.float32)
        grad_attended = jnp.where(valid, grad_attended, jnp.float32(0.0)).astype(jnp.bfloat16)

        def backward_block(carry, block):
            query_heads, key_heads, value_heads, allowed = gather_block(block)
            grad_block = split_heads(lax.dynamic_slice_in_dim(grad_attended, block * tok, tok, 0), head_count)
            grad_query, grad_key, grad_value = lax.map(lambda item: backward_head(*item),
                                                       (query_heads, key_heads, value_heads, allowed, grad_block))
            grad_pairs = jnp.stack([grad_key, grad_value], axis=2).transpose(1, 2, 0, 3).reshape(-1, 2, inner)
            for scale in range(SCALES):
                rate = 2 ** scale
                start = (block // rate) * rate * tok
                segment = spread(grad_pairs[scale * tok:(scale + 1) * tok], rate, head_count)
                current = lax.dynamic_slice_in_dim(carry, start, rate * tok, 0)
                carry = lax.dynamic_update_slice_in_dim(carry, current + segment, start, 0)
            return carry, grad_query.transpose(1, 0, 2).reshape(tok, inner)

        pair_grads, query_grads = lax.scan(backward_block, jnp.zeros((SEQ, 2, inner), jnp.float32), block_ids)
        grad_query = query_grads.reshape(SEQ, inner).astype(jnp.bfloat16)
        grad_key = pair_grads[:, 0].astype(jnp.bfloat16)
        grad_value = pair_grads[:, 1].astype(jnp.bfloat16)
        contract = (((1,), (1,)), ((), ()))
        grad_inputs = (lax.dot_general(grad_query, w_query, contract, preferred_element_type=jnp.float32)
                       + lax.dot_general(grad_key, w_key, contract, preferred_element_type=jnp.float32)
                       + lax.dot_general(grad_value, w_value, contract, preferred_element_type=jnp.float32))
        grad_list.append(grad_inputs.astype(jnp.bfloat16))
        grad_value_weight = grad_value_weight + lax.dot_general(inputs, grad_value, (((0,), (0,)), ((), ())), preferred_element_type=jnp.float32)
    return jnp.stack(mixed_list), jnp.stack(grad_list), grad_value_weight, grad_out_weight
```

```python
import functools

import jax
import jax.numpy as jnp
from jax import lax
from jax.experimental import pallas as pl
from jax.experimental.pallas import tpu as pltpu
from jax.sharding import Mesh, PartitionSpec as P

HEADS = 8
SCALES = 5
D = 768
INNER = 384
TOK = 128
DIM = INNER // HEADS
KEYS = SCALES * TOK
BF = jnp.bfloat16
F32 = jnp.float32
SLIDE = ("yl", "x")
ZY = ("z", "yh")
VMEM_LIMIT = 48 * 1024 * 1024


def dot(a, b):
    return jnp.dot(a, b, preferred_element_type=F32)


def dot_nt(a, b):
    return lax.dot_general(a, b, (((1,), (1,)), ((), ())), preferred_element_type=F32)


def dot_tn(a, b):
    return lax.dot_general(a, b, (((0,), (0,)), ((), ())), preferred_element_type=F32)


def partner(value, axis, mask):
    size = lax.axis_size(axis)
    return lax.ppermute(value, axis, [(source, source ^ mask) for source in range(size)])


def exchange(value, bit):
    axis, mask = (("c", 1), ("yh", 1), ("z", 1), ("z", 2))[bit]
    return partner(value, axis, mask)


def reversed4(value):
    return ((value & 1) << 3) | ((value & 2) << 1) | ((value & 4) >> 1) | ((value & 8) >> 3)


def row_position(row):
    return ((row & 7) << 4) + reversed4(row >> 3)


def swap_rows(rows):
    lane = lax.broadcasted_iota(jnp.int32, (1, rows.shape[1]), 1)
    head = jnp.zeros_like(lane)
    for start in range(DIM, rows.shape[1], DIM):
        head = head + (lane >= start).astype(jnp.int32)
    head = jnp.broadcast_to(head, rows.shape)
    for bit in range(3):
        size = 64 >> bit
        blocks = [rows[start : start + size] for start in range(0, TOK, size)]
        moved = jnp.concatenate([blocks[index ^ 1] for index in range(len(blocks))], 0)
        rows = jnp.where((head >> bit) & 1 == 1, moved, rows)
    return rows


def key_value_kernel(tokens_ref, own_ref, other_ref, out_ref):
    rows = dot(tokens_ref[:, :INNER], own_ref[...]) + dot(tokens_ref[:, INNER:], other_ref[...])
    out_ref[...] = swap_rows(rows).astype(BF)


def query_kernel(
    tokens_ref, grad_out_ref, valid_ref, order_ref, inner_ref, columns_ref, own_ref, other_ref,
    query_ref, upstream_ref, out_ref, pair_ref, query_weight_ref, joined,
):
    query = dot(tokens_ref[:, :INNER], own_ref[INNER:, :INNER])
    query = query + dot(tokens_ref[:, INNER:], other_ref[INNER:, :INNER])
    query_ref[...] = swap_rows(query).astype(BF)
    half = INNER // 2
    for place, part in enumerate((own_ref, other_ref)):
        for side in range(2):
            joined[place * half : (place + 1) * half, side * INNER : (side + 1) * INNER] = part[
                INNER + side * half : INNER + (side + 1) * half, INNER:
            ]
    out_weight = dot(inner_ref[...], joined[...]).astype(BF)
    out_ref[...] = out_weight
    upstream = dot_nt(grad_out_ref[...], out_weight)
    upstream = jnp.where(valid_ref[...] > 0, upstream, 0.0).astype(BF)
    upstream = dot(order_ref[...], upstream)
    upstream_ref[...] = swap_rows(upstream).astype(BF)
    columns = columns_ref[...]
    pair = dot(columns[:, :INNER], own_ref[:INNER, :]) + dot(columns[:, INNER:], other_ref[:INNER, :])
    pair_ref[...] = pair.astype(BF)
    weight = dot(columns[:, :INNER], own_ref[INNER:, :INNER])
    weight = weight + dot(columns[:, INNER:], other_ref[INNER:, :INNER])
    query_weight_ref[...] = weight.astype(BF)


def attention_kernel(
    query_ref, upstream_ref, rows_ref, h0, r0, h1, r1, h2, r2, h3, r3, position_ref, limit_ref,
    valid_ref, order_ref, inner_ref, out_weight_ref, grad_out_ref,
    mixed_ref, grad_query_ref, out_part_ref, grads_ref, pairs, attended, grad_query,
):
    scale = DIM ** -0.5
    pairs[:TOK, :] = rows_ref[...]
    for index, part in enumerate((h0, r0, h1, r1, h2, r2, h3, r3)):
        pairs[TOK + index * 64 : TOK + (index + 1) * 64, :] = part[...]
    limit = limit_ref[...]
    for head in range(HEADS):
        lanes = slice(head * DIM, (head + 1) * DIM)
        value_lanes = slice(INNER + head * DIM, INNER + (head + 1) * DIM)
        query = query_ref[:, lanes]
        upstream = upstream_ref[:, lanes]
        keys = pairs[:, lanes]
        values = pairs[:, value_lanes]
        position = position_ref[:1, :] ^ head
        probs_parts = []
        grad_parts = []
        out_parts = []
        grad_query_parts = []
        for start, count in ((0, KEYS), (64, TOK)):
            rows = slice(start, start + 64)
            scores = dot_nt(query[rows], keys[:count]) * scale
            allowed = jnp.broadcast_to(position[:, :count], (64, count)) < limit[rows, :count]
            scores = jnp.where(allowed, scores, jnp.float32(-1e9))
            expo = jnp.exp(scores - jnp.max(scores, axis=1, keepdims=True))
            probs = expo * (1.0 / jnp.sum(expo, axis=1, keepdims=True))
            weights = probs.astype(BF)
            out_parts.append(dot(weights, values[:count]))
            grad_probs = dot_nt(upstream[rows], values[:count])
            delta = jnp.sum(probs * grad_probs, axis=1, keepdims=True)
            grad_scores = (probs * (grad_probs - delta)).astype(BF)
            grad_query_parts.append(dot(grad_scores, keys[:count]) * scale)
            probs_parts.append(weights)
            grad_parts.append(grad_scores)
        attended[:, lanes] = jnp.concatenate(out_parts, 0)
        grad_query[:, lanes] = jnp.concatenate(grad_query_parts, 0)
        for left, right, target, factor in (
            (grad_parts, query, lanes, scale), (probs_parts, upstream, value_lanes, None)
        ):
            near = dot_tn(jnp.concatenate([left[0][:, :TOK], left[1]], 0), right)
            far = dot_tn(left[0][:, TOK:], right[:64])
            if factor is not None:
                near, far = near * factor, far * factor
            grads_ref[:TOK, target] = near
            grads_ref[TOK:, target] = far
    order = order_ref[...]
    rows = swap_rows(attended[...]).astype(BF)
    rows = jnp.where(valid_ref[...] > 0, dot_tn(order, rows), 0.0).astype(BF)
    mixed_ref[...] = dot(rows, out_weight_ref[...]).astype(BF)
    rows = dot(rows, inner_ref[...]).astype(BF)
    out_part_ref[...] = dot_tn(rows, grad_out_ref[...])
    rows = swap_rows(grad_query[...]).astype(BF)
    grad_query_ref[...] = dot_tn(order, rows).astype(BF)


def gradient_kernel(
    first_ref, total_ref, grad_query_ref, order_ref, tokens_ref, query_weight_ref, pair_ref,
    grad_tokens_ref, part_ref,
):
    rows = jnp.concatenate([first_ref[:64] + total_ref[...], first_ref[64:]], 0)
    rows = jnp.concatenate([swap_rows(rows[:, :INNER]), swap_rows(rows[:, INNER:])], 1).astype(BF)
    rows = dot_tn(order_ref[...], rows).astype(BF)
    part_ref[...] = dot_tn(tokens_ref[...], rows[:, INNER:])
    grads = dot_nt(grad_query_ref[...], query_weight_ref[...]) + dot_nt(rows, pair_ref[...])
    grad_tokens_ref[...] = grads.astype(BF)


def call(kernel, shapes, *operands, scratch=(), flops=0):
    return pl.pallas_call(
        kernel,
        out_shape=shapes,
        scratch_shapes=list(scratch),
        compiler_params=pltpu.CompilerParams(vmem_limit_bytes=VMEM_LIMIT),
        cost_estimate=pl.CostEstimate(flops=flops, bytes_accessed=4_000_000, transcendentals=0),
    )(*operands)


def shape(*sizes, kind=BF):
    return jax.ShapeDtypeStruct(sizes, kind)


def gather_weights(pair, rest):
    x = lax.axis_index("x")
    yl = lax.axis_index("yl")
    mine = jnp.where(yl == 0, pair, rest)
    mine = lax.dynamic_slice_in_dim(mine, x * 3, 3, 0)
    rows = lax.all_to_all(jnp.broadcast_to(mine[None], (32, 3, D)), ZY, 0, 0, tiled=True)
    rows = rows.reshape(1, 96, D)
    rows = lax.all_to_all(jnp.broadcast_to(rows, (8, 96, D)), SLIDE, 0, 0, tiled=True)
    rows = rows.reshape(D, D)
    return rows, partner(rows, "c", 1)


def reduce_weights(value_part, out_part):
    sent = jnp.concatenate([value_part[INNER:].reshape(-1, INNER), out_part[192:, :INNER], out_part[192:, INNER:]], 0)
    kept = jnp.concatenate([value_part[:INNER].reshape(-1, INNER), out_part[:192, :INNER], out_part[:192, INNER:]], 0)
    both = kept + partner(sent.astype(BF), "c", 1).astype(F32)
    pieces = lax.all_to_all(both.astype(BF).reshape(8, 96, INNER), SLIDE, 0, 0, tiled=True)
    piece = jnp.sum(pieces.astype(F32), 0)
    pieces = lax.all_to_all(piece.astype(BF).reshape(32, 3, INNER), ZY, 0, 0, tiled=True)
    piece = jnp.sum(pieces.astype(F32), 0)
    full = lax.all_to_all(jnp.broadcast_to(piece[None], (8, 3, INNER)), SLIDE, 0, 0, tiled=True)
    value_share = full[:4].reshape(12, INNER)
    out_share = jnp.concatenate([full[4:6].reshape(6, INNER), full[6:].reshape(6, INNER)], 1)
    return value_share, out_share


def first_halves(rows, count):
    size = rows.shape[0] // count
    return rows.reshape(count, size, -1)[:, : size // 2].reshape(rows.shape[0] // 2, -1)


def on_device(tokens, lengths, w_query, w_key, w_value, w_out, grad_out):
    inputs, grad_out, length = tokens[0], grad_out[0], lengths[0]
    core = lax.axis_index("c")
    block = (lax.axis_index("z") * 2 + lax.axis_index("yh")) * 2 + core

    pair = jnp.concatenate([w_key, w_value], 1)
    rest = jnp.concatenate([w_query, jnp.concatenate([w_out[:, :INNER], w_out[:, INNER:]], 0)], 1)
    own, other = gather_weights(pair, rest)

    row = jnp.arange(TOK, dtype=jnp.int32)
    order = (row_position(row)[:, None] == row[None, :]).astype(BF)
    column = jnp.arange(D, dtype=jnp.int32)
    place, left = column // INNER, column % INNER
    source = left % 96 // 3 * 24 + (core ^ place) * 12 + left // 96 * 3 + left % 3
    columns = (column[:, None] == source[None, :]).astype(BF)
    column = jnp.arange(INNER, dtype=jnp.int32)
    place, left = column // 192, column % 192
    source = left % 96 // 3 * 12 + (core ^ place) * 6 + left // 96 * 3 + left % 3
    inner = (column[:, None] == source[None, :]).astype(BF)
    valid = (block * TOK + row < length).astype(F32)[:, None]

    parts, limits = [], []
    for scale in range(SCALES):
        size = TOK >> scale
        parts.append((block ^ (row // size)) * TOK + row_position(row % size))
        limits.append(jnp.where(row[:, None] < size, length, -1) + jnp.zeros((1, TOK), jnp.int32))
    position = jnp.broadcast_to(jnp.concatenate(parts)[None], (8, KEYS))
    limit = jnp.concatenate(limits, 1)

    tokens_columns = dot(inputs, columns).astype(BF)
    tokens_rows = dot(order, tokens_columns).astype(BF)

    rows = pl.pallas_call(
        key_value_kernel,
        grid=(1,),
        in_specs=[
            pl.BlockSpec((TOK, D), lambda i: (0, 0)),
            pl.BlockSpec((INNER, D), lambda i: (0, 0)),
            pl.BlockSpec((INNER, D), lambda i: (0, 0)),
        ],
        out_specs=pl.BlockSpec((TOK, D), lambda i: (0, 0)),
        out_shape=shape(TOK, D),
        compiler_params=pltpu.CompilerParams(vmem_limit_bytes=VMEM_LIMIT),
    )(tokens_rows, own, other)

    halves, received = [], []
    current = rows
    for bit in range(SCALES - 1):
        half = first_halves(current, 1 << bit)
        got = exchange(half, bit)
        halves.append(half)
        received.append(got)
        current = jnp.concatenate([half, got], 0)

    query, upstream, out_weight, pair_weight, query_weight = call(
        query_kernel,
        (shape(TOK, INNER), shape(TOK, INNER), shape(INNER, D), shape(D, D), shape(D, INNER)),
        tokens_rows, grad_out, valid, order, inner, columns, own, other,
        scratch=[pltpu.VMEM((INNER, D), BF)],
        flops=3_000_000_000,
    )

    exchanged = [part for both in zip(halves, received) for part in both]
    mixed, grad_query, out_part, grads = call(
        attention_kernel,
        (shape(TOK, D), shape(TOK, INNER), shape(INNER, D, kind=F32), shape(KEYS, D, kind=F32)),
        query, upstream, rows, *exchanged, position, limit, valid, order, inner, out_weight, grad_out,
        scratch=[pltpu.VMEM((KEYS, D), BF), pltpu.VMEM((TOK, INNER), F32), pltpu.VMEM((TOK, INNER), F32)],
        flops=3_000_000_000,
    )

    total = None
    for scale in range(SCALES - 1, 0, -1):
        current = grads[scale * TOK : (scale + 1) * TOK]
        if total is not None:
            count = 1 << scale
            size = TOK // count
            current = current.reshape(count, size, D)
            added = current[:, : size // 2] + total.reshape(count, size // 2, D)
            current = jnp.concatenate([added, current[:, size // 2 :]], 1).reshape(TOK, D)
        total = current[:64] + exchange(current[64:].astype(BF), scale - 1).astype(F32)

    grad_tokens, value_part = call(
        gradient_kernel,
        (shape(TOK, D), shape(D, INNER, kind=F32)),
        grads[:TOK], total, grad_query, order, tokens_columns, query_weight, pair_weight,
    )
    value_share, out_share = reduce_weights(value_part, out_part)
    return mixed[None], grad_tokens[None], value_share, out_share


def solution(mesh):
    fine = Mesh(mesh.devices.reshape(2, 4, 16, 2, 2), ("yl", "x", "z", "yh", "c"))
    seq = ("z", "yh", "c")
    rows = P(seq, None)
    whole = P(SLIDE, seq, None)
    return jax.shard_map(
        on_device,
        mesh=fine,
        in_specs=(whole, P(SLIDE), rows, rows, rows, rows, whole),
        out_specs=(whole, whole, rows, rows),
        check_vma=False,
    )
```

```python
import jax
import jax.numpy as jnp
from jax import lax
from jax.experimental import pallas as pl
from jax.experimental.pallas import tpu as pltpu
from jax.sharding import Mesh, PartitionSpec as P

SCALES = 5
D = 768
INNER = 384
TOK = 128
PAIR = 2 * TOK
DIM = 48
LOCAL_HEADS = 4
HALF = LOCAL_HEADS * DIM
FAR = (SCALES - 1) * TOK
BF = jnp.bfloat16
F32 = jnp.float32
SLIDE = ("yl", "x")
Z = ("zh", "zl")
NEAR = ("zl", "yh")
PLANE = ("yl", "x", "yh", "c")
VMEM_LIMIT = 60 * 1024 * 1024


def dot(a, b):
    return jnp.dot(a, b, preferred_element_type=F32)


def dot_nt(a, b):
    return lax.dot_general(a, b, (((1,), (1,)), ((), ())), preferred_element_type=F32)


def dot_tn(a, b):
    return lax.dot_general(a, b, (((0,), (0,)), ((), ())), preferred_element_type=F32)


def partner(value, axis):
    return lax.ppermute(value, axis, [(0, 1), (1, 0)])


def reversed4(value):
    return ((value & 1) << 3) | ((value & 2) << 1) | ((value & 4) >> 1) | ((value & 8) >> 3)


def swap_rows(rows):
    lane = lax.broadcasted_iota(jnp.int32, (1, rows.shape[1]), 1)
    head = jnp.zeros_like(lane)
    for start in range(DIM, rows.shape[1], DIM):
        head = head + (lane >= start).astype(jnp.int32)
    head = jnp.broadcast_to(head, rows.shape)
    for bit in range(2):
        size = 128 >> bit
        blocks = [rows[start : start + size] for start in range(0, PAIR, size)]
        moved = jnp.concatenate([blocks[index ^ 1] for index in range(len(blocks))], 0)
        rows = jnp.where((head >> bit) & 1 == 1, moved, rows)
    return rows


def to_mixed(rows):
    return jnp.concatenate(
        [rows[block * TOK + group * 8 :][:8] for group in range(16) for block in range(2)], 0
    )


def to_split(rows):
    return jnp.concatenate(
        [rows[group * 16 + block * 8 :][:8] for block in range(2) for group in range(16)], 0
    )


def key_value_kernel(tokens_ref, weight_ref, mixed_ref, split_ref):
    rows = swap_rows(dot(tokens_ref[...], weight_ref[...]))
    mixed_ref[...] = rows.astype(BF)
    split_ref[...] = to_split(rows).astype(BF)


def query_kernel(
    low_ref, high_ref, grad_out_ref, valid_ref, order_ref, pick_ref, rest_ref,
    query_ref, query_split_ref, upstream_ref, upstream_split_ref, out_ref,
):
    query = dot(low_ref[...], rest_ref[:, :HALF]) + dot(high_ref[...], rest_ref[:, HALF:])
    query = swap_rows(query)
    query_ref[...] = query[:TOK].astype(BF)
    query_split_ref[...] = to_split(query).astype(BF)
    pick = pick_ref[...]
    out_weight = jnp.concatenate([dot(pick, rest_ref[:INNER, :]), dot(pick, rest_ref[INNER:, :])], 1)
    out_weight = out_weight.astype(BF)
    out_ref[...] = out_weight
    upstream = dot_nt(grad_out_ref[...], out_weight)
    upstream = jnp.where(valid_ref[...] > 0, upstream, 0.0).astype(BF)
    upstream = swap_rows(dot(order_ref[...], upstream))
    upstream_ref[...] = upstream[:TOK].astype(BF)
    upstream_split_ref[...] = to_split(upstream).astype(BF)


def attention_kernel(
    scalar_ref, query_ref, query_split_ref, upstream_ref, upstream_split_ref, split_ref, rows_ref,
    beside_ref, around_ref, near_position_ref, far_position_ref, limit_ref, valid_ref, order_ref,
    inner_ref, out_weight_ref, grad_out_ref,
    mixed_ref, grad_query_ref, out_part_ref, near_ref, beside_out_ref, around_out_ref,
    far_rows, far_ref, wide, attended, grad_query,
):
    scale = DIM ** -0.5
    length, start = scalar_ref[0], scalar_ref[1]
    far_rows[:TOK, :] = rows_ref[:TOK, :]
    far_rows[TOK : TOK + 64, :] = rows_ref[:64, :]
    far_rows[TOK + 64 : PAIR, :] = beside_ref[...]
    far_rows[PAIR : PAIR + TOK, :] = around_ref[pl.ds(start, 4)].reshape(TOK, INNER)
    far_rows[PAIR + TOK :, :] = around_ref[:, :16, :].reshape(TOK, INNER)
    limit = limit_ref[...]
    heads = range(LOCAL_HEADS)
    lanes = [slice(h * DIM, (h + 1) * DIM) for h in heads]
    value_lanes = [slice(HALF + h * DIM, HALF + (h + 1) * DIM) for h in heads]
    blocks = [slice(0, TOK), slice(TOK, PAIR)]

    near_scores, far_scores = [], []
    for h in heads:
        parts = []
        for b, rows in enumerate(blocks):
            scores = dot_nt(query_split_ref[rows, lanes[h]], split_ref[rows, lanes[h]]) * scale
            position = near_position_ref[b : b + 1, :] ^ h
            parts.append(jnp.where(position < length, scores, jnp.float32(-1e9)))
        near_scores.append(to_mixed(jnp.concatenate(parts, 0)))
        scores = dot_nt(query_ref[:, lanes[h]], far_rows[:, lanes[h]]) * scale
        position = far_position_ref[:1, :] ^ h
        far_scores.append(
            jnp.where(jnp.broadcast_to(position, scores.shape) < limit, scores, jnp.float32(-1e9))
        )
    near_grads, far_grads = [], []
    for h in heads:
        parts = [dot_nt(upstream_split_ref[rows, lanes[h]], split_ref[rows, value_lanes[h]]) for rows in blocks]
        near_grads.append(to_mixed(jnp.concatenate(parts, 0)))
        far_grads.append(dot_nt(upstream_ref[:, lanes[h]], far_rows[:, value_lanes[h]]))

    near_weights, far_weights, near_steps, far_steps = [], [], [], []
    for h in heads:
        top = jnp.max(near_scores[h], axis=1, keepdims=True)
        far_top = jnp.maximum(top[:TOK], jnp.max(far_scores[h], axis=1, keepdims=True))
        top = jnp.concatenate([far_top, top[TOK:]], 0)
        near = jnp.exp(near_scores[h] - top)
        far = jnp.exp(far_scores[h] - far_top)
        total = jnp.sum(near, axis=1, keepdims=True)
        total = jnp.concatenate([total[:TOK] + jnp.sum(far, axis=1, keepdims=True), total[TOK:]], 0)
        factor = 1.0 / total
        near = near * factor
        far = far * factor[:TOK]
        delta = jnp.sum(near * near_grads[h], axis=1, keepdims=True)
        far_delta = delta[:TOK] + jnp.sum(far * far_grads[h], axis=1, keepdims=True)
        delta = jnp.concatenate([far_delta, delta[TOK:]], 0)
        near_weights.append(to_split(near).astype(BF))
        far_weights.append(far.astype(BF))
        near_steps.append(to_split(near * (near_grads[h] - delta)).astype(BF))
        far_steps.append((far * (far_grads[h] - far_delta)).astype(BF))

    for h in heads:
        for target, near, far, source in (
            (attended, near_weights[h], far_weights[h], value_lanes[h]),
            (grad_query, near_steps[h], far_steps[h], lanes[h]),
        ):
            rows = jnp.concatenate([dot(near[b], split_ref[b, source]) for b in blocks], 0)
            rows = to_mixed(rows)
            far_part = dot(far, far_rows[:, source])
            rows = jnp.concatenate([rows[:TOK] + far_part, rows[TOK:]], 0)
            target[:, lanes[h]] = rows if target is attended else rows * scale
        for near, far, right, near_right, target, factor in (
            (near_steps[h], far_steps[h], query_ref, query_split_ref, lanes[h], scale),
            (near_weights[h], far_weights[h], upstream_ref, upstream_split_ref, value_lanes[h], 1.0),
        ):
            rows = jnp.concatenate([dot_tn(near[b], near_right[b, lanes[h]]) for b in blocks], 0)
            near_ref[:, target] = to_mixed(rows) * factor
            far_ref[:, target] = dot_tn(far, right[:, lanes[h]]) * factor

    near_ref[:64, :] += far_ref[:64, :] + far_ref[TOK : TOK + 64, :]
    near_ref[64:TOK, :] += far_ref[64:TOK, :]
    beside_out_ref[...] = far_ref[TOK + 64 : PAIR, :].astype(BF)
    wide[:, :16, :] = far_ref[PAIR + TOK :, :].reshape(8, 16, INNER)
    wide[:, 16:, :] = jnp.zeros((8, 16, INNER), F32)
    wide[pl.ds(start, 4)] += far_ref[PAIR : PAIR + TOK, :].reshape(4, 32, INNER)
    around_out_ref[...] = wide[...].astype(BF)

    order = order_ref[...]
    rows = swap_rows(attended[...]).astype(BF)
    rows = jnp.where(valid_ref[...] > 0, dot_tn(order, rows), 0.0).astype(BF)
    mixed_ref[...] = dot(rows, out_weight_ref[...])
    rows = dot(rows, inner_ref[...]).astype(BF)
    part = dot_tn(rows, grad_out_ref[...]).astype(BF)
    out_part_ref[:HALF, :] = part[:, :INNER]
    out_part_ref[HALF:, :] = part[:, INNER:]
    rows = swap_rows(grad_query[...]).astype(BF)
    grad_query_ref[...] = dot_tn(order, rows).astype(BF)


def value_kernel(
    near_ref, beside_ref, around_ref, order_ref, low_ref, high_ref, out_part_ref, rows_ref, part_ref
):
    first = jnp.sum(around_ref[...].astype(F32), 0)
    rows = near_ref[...]
    beside = rows[:64] + beside_ref[...].astype(F32)
    rows = jnp.concatenate([beside[:32] + first, beside[32:], rows[64:]], 0)
    rows = dot_tn(order_ref[...], swap_rows(rows).astype(BF)).astype(BF)
    rows_ref[...] = rows
    part_ref[:INNER, :HALF] = dot_tn(low_ref[...], rows[:, HALF:]).astype(BF)
    part_ref[:INNER, HALF:] = dot_tn(high_ref[...], rows[:, HALF:]).astype(BF)
    part_ref[INNER:, :] = out_part_ref[...]


def tokens_kernel(
    grad_query_ref, rows_ref, columns_ref, low_columns_ref, high_columns_ref, pair_ref, rest_ref, out_ref
):
    pair = dot(columns_ref[...], pair_ref[...]).astype(BF)
    weight = dot(low_columns_ref[...], rest_ref[:, :HALF])
    weight = (weight + dot(high_columns_ref[...], rest_ref[:, HALF:])).astype(BF)
    out_ref[...] = dot_nt(grad_query_ref[...], weight) + dot_nt(rows_ref[...], pair)


def call(kernel, shapes, *operands, scratch=(), flops=0, special={}):
    def whole(leaf):
        return pl.BlockSpec(leaf.shape, lambda step: (0,) * len(leaf.shape))

    specs = [special.get(index) or whole(leaf) for index, leaf in enumerate(operands)]
    return pl.pallas_call(
        kernel,
        grid=(1,),
        out_shape=shapes,
        in_specs=specs,
        out_specs=jax.tree.map(whole, shapes),
        scratch_shapes=list(scratch),
        compiler_params=pltpu.CompilerParams(vmem_limit_bytes=VMEM_LIMIT),
        cost_estimate=pl.CostEstimate(flops=flops, bytes_accessed=4_000_000, transcendentals=0),
    )(*operands)


PAIR_WEIGHT = pl.BlockSpec((D, INNER), lambda step: (0, 0))
REST_WEIGHT = pl.BlockSpec((D, INNER), lambda step: (1, 0))


def shape(*sizes, kind=BF):
    return jax.ShapeDtypeStruct(sizes, kind)


def gather_weights(w_query, w_key, w_value, w_out):
    yl, x = lax.axis_index("yl"), lax.axis_index("x")
    mine = None
    for index in range(4):
        rows, side = slice(3 * index, 3 * index + 3), slice((index >> 1) * INNER, (index >> 1) * INNER + INNER)
        out_rows = slice((index & 1) * 3, (index & 1) * 3 + 3)
        part = jnp.concatenate(
            [
                jnp.where(yl == 0, w_key[rows], w_query[rows]),
                jnp.where(yl == 0, w_value[rows], w_out[out_rows, side]),
            ],
            1,
        )
        mine = part if mine is None else jnp.where(x == index, part, mine)
    rows = lax.all_to_all(jnp.broadcast_to(mine[None], (16, 3, D)), Z, 0, 0, tiled=True)
    rows = rows.reshape(48, D)
    left, right = rows[:, :INNER], rows[:, INNER:]
    chunks = []
    for core in range(2):
        lanes = slice(core * HALF, (core + 1) * HALF)
        both = jnp.concatenate([left[:, lanes], right[:, lanes]], 1)
        query = jnp.concatenate([left[:24, lanes], left[24:, lanes]], 1)
        other = jnp.concatenate([query, right[core * 24 : (core + 1) * 24]], 0)
        chunks.append(jnp.where(yl == 0, both, other))
    chunks = jnp.broadcast_to(jnp.stack(chunks)[None], (16, 2, 48, INNER)).reshape(32, 48, INNER)
    return rows, lax.all_to_all(chunks, PLANE, 0, 0, tiled=True).reshape(2 * D, INNER)


def reduce_weights(part):
    pieces = lax.all_to_all(part.reshape(32, 24, INNER), PLANE, 0, 0, tiled=True).reshape(16, 2, 24, INNER)
    piece = jnp.sum(pieces.astype(F32), 0)
    value = jnp.stack(
        [jnp.concatenate([piece[0, :, lanes], piece[1, :, lanes]], 1) for lanes in (slice(0, HALF), slice(HALF, INNER))]
    )
    piece = jnp.where(lax.axis_index("yl") == 0, value, piece).astype(BF).reshape(16, 3, INNER)
    piece = jnp.sum(lax.all_to_all(piece, Z, 0, 0, tiled=True).astype(F32), 0)
    full = lax.all_to_all(jnp.broadcast_to(piece[None], (8, 3, INNER)), SLIDE, 0, 0, tiled=True)
    value_share = full[:4].reshape(12, INNER)
    out_share = jnp.concatenate([full[4:6].reshape(6, INNER), full[6:].reshape(6, INNER)], 1)
    return value_share, out_share


def one_hot(source, size):
    return (jnp.arange(size, dtype=jnp.int32)[:, None] == source[None, :]).astype(BF)


def on_device(tokens, lengths, w_query, w_key, w_value, w_out, grad_out):
    length = lengths[0]
    core, yh = lax.axis_index("c"), lax.axis_index("yh")
    zh, zl = lax.axis_index("zh"), lax.axis_index("zl")
    block = ((zh * 4 + zl) * 2 + yh) * 2 + core

    gathered, weights = gather_weights(w_query, w_key, w_value, w_out)

    own, gathered = lax.optimization_barrier((jnp.concatenate([tokens[0], grad_out[0]], 0), gathered))
    other = partner(own, "c")
    inputs = jnp.concatenate([own[:TOK], other[:TOK]], 0)
    upstream_rows = jnp.concatenate([own[TOK:], other[TOK:]], 0)

    row = jnp.arange(PAIR, dtype=jnp.int32)
    group, which = row >> 4, (row >> 3) & 1
    within = ((row & 7) << 4) + (reversed4(group) ^ (core * 4))
    order = one_hot(which * TOK + within, PAIR).T
    valid = ((block ^ (row >> 7)) * TOK + (row & 127) < length).astype(F32)[:, None]

    column = jnp.arange(D, dtype=jnp.int32)
    place, left = column // 48, column % 48
    x, middle = place >> 2, place & 3
    columns = one_hot((left // 3 * 4 + middle) * 12 + x * 3 + left % 3, D)
    low = (left // 3 * 4 + middle) * 12 + x * 3 + left % 3
    low_columns = one_hot(jnp.where(left < 24, low, -1), D)
    high_columns = one_hot(jnp.where(left < 24, low + 8 * 48, -1), D)
    column = jnp.arange(INNER, dtype=jnp.int32)
    place, left = column // 24, column % 24
    low = (left // 3 * 4 + (place & 3)) * 12 + (place >> 2) * 3 + left % 3
    low_short, high_short = one_hot(low, D), one_hot(low + 8 * 48, D)
    column = jnp.arange(HALF, dtype=jnp.int32)
    place, left = column // 24, column % 24
    inner = one_hot((left // 3 * 4 + (place & 3)) * 6 + (place >> 2) * 3 + left % 3, HALF)
    column = jnp.arange(INNER, dtype=jnp.int32)
    place, left = column // 48, column % 48 - 24
    source = (left // 3 * 4 + (place & 3)) * 6 + (place >> 2) * 3 + left % 3
    pick = one_hot(jnp.where(left >= 0, source, -1), HALF)

    def key_position(member, size):
        place = row[:size]
        return ((member ^ which[:size]) * TOK) + within[:size]

    near_position = jnp.stack([(block ^ b) * TOK + ((row[:TOK] & 7) << 4) + (reversed4(row[:TOK] >> 3) ^ (core * 4)) for b in range(2)])
    near_position = jnp.concatenate([near_position] * 4, 0)
    parts = [key_position(block, 128), key_position(block, 64), key_position(block ^ 2, 64)]
    start = (zl >> 1) * 2
    for member in range(4):
        parts.append(key_position(((zh * 4 + start + (member >> 1)) * 2 + (member & 1)) * 2 + core, 32))
    for member in range(8):
        parts.append(key_position(((zh * 4 + (member >> 1)) * 2 + (member & 1)) * 2 + core, 16))
    far_position = jnp.broadcast_to(jnp.concatenate(parts)[None], (8, FAR))
    limit = jnp.concatenate(
        [jnp.where(row[:TOK, None] < (PAIR >> scale), length, -1) + jnp.zeros((1, TOK), jnp.int32) for scale in range(1, SCALES)], 1
    )

    tokens_rows = dot(order, inputs).astype(BF)
    tokens_pair = dot(tokens_rows, columns).astype(BF)
    tokens_low, tokens_high = dot(tokens_rows, low_columns).astype(BF), dot(tokens_rows, high_columns).astype(BF)
    inputs_low, inputs_high = dot(inputs, low_short).astype(BF), dot(inputs, high_short).astype(BF)

    prepared = (
        upstream_rows, order, valid, columns, low_columns, high_columns, inner, pick, near_position, far_position,
        limit, tokens_pair, tokens_low, tokens_high, inputs_low, inputs_high,
    )
    (
        upstream_rows, order, valid, columns, low_columns, high_columns, inner, pick, near_position, far_position,
        limit, tokens_pair, tokens_low, tokens_high, inputs_low, inputs_high,
    ) = lax.optimization_barrier(prepared)

    rows, rows_split = call(
        key_value_kernel, (shape(PAIR, INNER), shape(PAIR, INNER)), tokens_pair, weights,
        special={1: PAIR_WEIGHT},
        flops=200_000_000,
    )
    around = lax.all_to_all(jnp.broadcast_to(rows[None, :32], (8, 32, INNER)), NEAR, 0, 0, tiled=True)
    beside = partner(rows[:64], "yh")

    query, query_split, upstream, upstream_split, out_weight = call(
        query_kernel,
        (shape(TOK, HALF), shape(PAIR, HALF), shape(TOK, HALF), shape(PAIR, HALF), shape(HALF, D)),
        tokens_low, tokens_high, upstream_rows, valid, order, pick, weights,
        special={6: REST_WEIGHT},
        flops=3_000_000_000,
    )

    scalars = jnp.stack([length, (zl >> 1) * 4]).astype(jnp.int32)
    mixed, grad_query, out_part, near_grads, beside, around = call(
        attention_kernel,
        (
            shape(PAIR, D, kind=F32), shape(PAIR, HALF), shape(INNER, INNER),
            shape(PAIR, INNER, kind=F32), shape(64, INNER), shape(8, 32, INNER),
        ),
        scalars, query, query_split, upstream, upstream_split, rows_split, rows, beside, around,
        near_position, far_position, limit, valid, order, inner, out_weight, upstream_rows,
        scratch=[
            pltpu.VMEM((FAR, INNER), BF), pltpu.VMEM((FAR, INNER), F32), pltpu.VMEM((8, 32, INNER), F32),
            pltpu.VMEM((PAIR, HALF), F32), pltpu.VMEM((PAIR, HALF), F32),
        ],
        special={0: pl.BlockSpec(memory_space=pltpu.SMEM)},
        flops=3_000_000_000,
    )

    around = lax.all_to_all(around, NEAR, 0, 0, tiled=True)
    beside = partner(beside, "yh")
    grad_rows, part = call(
        value_kernel,
        (shape(PAIR, INNER), shape(D, INNER)),
        near_grads, beside, around, order, inputs_low, inputs_high, out_part,
        flops=200_000_000,
    )
    value_share, out_share = reduce_weights(part)
    grad_tokens = call(
        tokens_kernel, shape(PAIR, D, kind=F32), grad_query, grad_rows, columns, low_columns, high_columns,
        weights, weights,
        special={5: PAIR_WEIGHT, 6: REST_WEIGHT},
        flops=3_000_000_000,
    )
    mixed = (mixed[:TOK] + partner(mixed[TOK:], "c")).astype(BF)
    grad_tokens = (grad_tokens[:TOK] + partner(grad_tokens[TOK:], "c")).astype(BF)
    return mixed[None], grad_tokens[None], value_share, out_share


def solution(mesh):
    fine = Mesh(mesh.devices.reshape(2, 4, 4, 4, 2, 2), ("yl", "x", "zh", "zl", "yh", "c"))
    seq = ("zh", "zl", "yh", "c")
    rows = P(seq, None)
    whole = P(SLIDE, seq, None)
    return jax.shard_map(
        on_device,
        mesh=fine,
        in_specs=(whole, P(SLIDE), rows, rows, rows, rows, whole),
        out_specs=(whole, whole, rows, rows),
        check_vma=False,
    )
```

```python
import jax
import jax.numpy as jnp
from jax import lax
from jax.experimental import pallas as pl
from jax.experimental.pallas import tpu as pltpu
from jax.sharding import Mesh, PartitionSpec as P

D = 768
INNER = 384
TOK = 128
QUAD = 4 * TOK
DIM = 48
LOCAL_HEADS = 2
PART = LOCAL_HEADS * DIM
FAR = 3 * TOK
BF = jnp.bfloat16
F32 = jnp.float32
SLIDE = ("yl", "x")
Z = ("zh", "zl")
PLANE = ("yl", "x", "yh", "c")
VMEM_LIMIT = 60 * 1024 * 1024

SPLIT_TO_MIXED = [m * 128 + g * 8 for g in range(16) for m in range(4)]
MIXED_TO_SPLIT = [g * 32 + m * 8 for m in range(4) for g in range(16)]
PAIR_TO_MIXED = [(m >> 1) * 128 + g * 16 + (m & 1) * 8 for g in range(8) for m in range(4)]
MIXED_TO_PAIR = [g * 32 + (p * 2 + c) * 8 for p in range(2) for g in range(8) for c in range(2)]


def dot(a, b):
    return jnp.dot(a, b, preferred_element_type=F32)


def dot_nt(a, b):
    return lax.dot_general(a, b, (((1,), (1,)), ((), ())), preferred_element_type=F32)


def dot_tn(a, b):
    return lax.dot_general(a, b, (((0,), (0,)), ((), ())), preferred_element_type=F32)


def partner(value, axis):
    return lax.ppermute(value, axis, [(0, 1), (1, 0)])


def reversed4(value):
    return ((value & 1) << 3) | ((value & 2) << 1) | ((value & 4) >> 1) | ((value & 8) >> 3)


def regroup(rows, starts):
    return jnp.concatenate([rows[start : start + 8] for start in starts], 0)


def swap_rows(rows):
    lane = lax.broadcasted_iota(jnp.int32, rows.shape, 1)
    odd = (lane >= DIM) & (lane < 2 * DIM) | (lane >= 3 * DIM)
    moved = jnp.concatenate([rows[QUAD // 2 :], rows[: QUAD // 2]], 0)
    return jnp.where(odd, moved, rows)


def first_kernel(key_ref, value_ref, query_ref, out_weight_ref, out_ref):
    yl, x = lax.axis_index("yl"), lax.axis_index("x")
    query, key, value = (ref[...].astype(F32) for ref in (query_ref, key_ref, value_ref))
    out_weight = out_weight_ref[...].astype(F32)
    left = jnp.where(yl == 0, key, query)
    mine = None
    for index in range(4):
        rows = slice(3 * index, 3 * index + 3)
        out_rows = slice((index & 1) * 3, (index & 1) * 3 + 3)
        side = slice((index >> 1) * INNER, (index >> 1) * INNER + INNER)
        right = jnp.where(yl == 0, value[rows], out_weight[out_rows, side])
        part = jnp.concatenate([left[rows], right], 1)
        mine = part if mine is None else jnp.where(x == index, part, mine)
    out_ref[...] = jnp.broadcast_to(mine.astype(BF)[None], out_ref.shape)


def chunk_kernel(pieces_ref, out_ref, joined):
    yl = lax.axis_index("yl")
    for index in range(16):
        joined[3 * index : 3 * index + 3, :] = pieces_ref[index].astype(F32)
    rows = joined[...]
    for member in range(4):
        lanes = slice(member * PART, (member + 1) * PART)
        other = rows[member * 12 : (member + 1) * 12, INNER:]
        other = jnp.concatenate([other[:, q * PART : (q + 1) * PART] for q in range(4)], 0)
        right = jnp.where(yl == 0, rows[:, INNER:][:, lanes], other)
        chunk = jnp.concatenate([rows[:, lanes], right], 1).astype(BF)
        for place in range(8):
            out_ref[place, member] = chunk


def key_value_kernel(tokens_ref, weight_ref, split_ref, pair_ref, near_ref, sent_ref):
    rows = swap_rows(dot(tokens_ref[...], weight_ref[...]))
    split_ref[...] = regroup(rows, MIXED_TO_SPLIT).astype(BF)
    pair_ref[...] = regroup(rows, MIXED_TO_PAIR).astype(BF)
    near = rows[:TOK].astype(BF)
    near_ref[...] = near
    for member in range(4):
        sent_ref[member] = near[:64]


def query_kernel(
    tokens_ref, grad_out_ref, valid_ref, order_ref, pick_ref, rest_ref,
    query_split_ref, query_pair_ref, query_ref, upstream_split_ref, upstream_pair_ref, upstream_ref, out_ref,
):
    def store(rows, split_ref, pair_ref, near_ref):
        split_ref[...] = regroup(rows, MIXED_TO_SPLIT).astype(BF)
        pair_ref[...] = regroup(rows, MIXED_TO_PAIR).astype(BF)
        near_ref[...] = rows[:TOK].astype(BF)

    rest = rest_ref[...]
    query = swap_rows(dot(tokens_ref[...], rest[:, :PART]))
    store(query, query_split_ref, query_pair_ref, query_ref)
    blocks = []
    for side in range(2):
        block = dot(pick_ref[...], rest[side * INNER : (side + 1) * INNER, PART:])
        blocks += [block[q * PART : (q + 1) * PART] for q in range(4)]
    out_weight = jnp.concatenate(blocks, 1).astype(BF)
    out_ref[...] = out_weight
    upstream = dot_nt(grad_out_ref[...], out_weight)
    upstream = jnp.where(valid_ref[...] > 0, upstream, 0.0).astype(BF)
    upstream = swap_rows(dot(order_ref[...], upstream))
    store(upstream, upstream_split_ref, upstream_pair_ref, upstream_ref)


def attention_kernel(
    length_ref, query_split_ref, query_pair_ref, query_ref, upstream_split_ref, upstream_pair_ref, upstream_ref,
    split_ref, pair_ref, rows_ref, around_ref, near_position_ref, far_position_ref, limit_ref,
    attended_ref, grad_query_ref, near_ref, around_out_ref, far_rows, far_ref, wide, attended, grad_query,
):
    scale = DIM ** -0.5
    length, start = length_ref[0], (lax.axis_index("zl") >> 1) * 2
    far_rows[:TOK, :] = rows_ref[...]
    far_rows[TOK : 2 * TOK, :] = around_ref[pl.ds(start, 2)].reshape(TOK, 2 * PART)
    far_rows[2 * TOK :, :] = around_ref[:, :32, :].reshape(TOK, 2 * PART)
    limit = limit_ref[...]
    heads = range(LOCAL_HEADS)
    lanes = [slice(h * DIM, (h + 1) * DIM) for h in heads]
    value_lanes = [slice(PART + h * DIM, PART + (h + 1) * DIM) for h in heads]
    blocks = [slice(m * TOK, (m + 1) * TOK) for m in range(4)]
    pairs = blocks[:2]

    def grow(low, high, combine):
        size = low.shape[0]
        return jnp.concatenate([combine(high[:size], low), high[size:]], 0)

    scores, grads = [], []
    for h in heads:
        def masked(query, keys, position):
            position = position ^ h
            return jnp.where(position < length, dot_nt(query, keys) * scale, jnp.float32(-1e9))

        s0 = [masked(query_split_ref[b, lanes[h]], split_ref[b, lanes[h]], near_position_ref[m : m + 1, :]) for m, b in enumerate(blocks)]
        s1 = [masked(query_pair_ref[b, lanes[h]], pair_ref[b, lanes[h]], near_position_ref[4 + p : 5 + p, :]) for p, b in enumerate(pairs)]
        s2 = dot_nt(query_ref[:, lanes[h]], far_rows[:, lanes[h]]) * scale
        position = jnp.broadcast_to(far_position_ref[:1, :] ^ h, s2.shape)
        s2 = jnp.where(position < limit, s2, jnp.float32(-1e9))
        scores.append(
            [regroup(jnp.concatenate(s0, 0), SPLIT_TO_MIXED), regroup(jnp.concatenate(s1, 0), PAIR_TO_MIXED), s2]
        )
    for h in heads:
        g0 = [dot_nt(upstream_split_ref[b, lanes[h]], split_ref[b, value_lanes[h]]) for b in blocks]
        g1 = [dot_nt(upstream_pair_ref[b, lanes[h]], pair_ref[b, value_lanes[h]]) for b in pairs]
        g2 = dot_nt(upstream_ref[:, lanes[h]], far_rows[:, value_lanes[h]])
        grads.append(
            [regroup(jnp.concatenate(g0, 0), SPLIT_TO_MIXED), regroup(jnp.concatenate(g1, 0), PAIR_TO_MIXED), g2]
        )

    weights, steps = [], []
    for h in heads:
        def rows_of(values, reduce, combine):
            total = reduce(values[2], axis=1, keepdims=True)
            for value in (values[1], values[0]):
                total = grow(total, reduce(value, axis=1, keepdims=True), combine)
            return total

        top = rows_of(scores[h], jnp.max, jnp.maximum)
        expo = [jnp.exp(s - top[: s.shape[0]]) for s in scores[h]]
        factor = 1.0 / rows_of(expo, jnp.sum, jnp.add)
        probs = [e * factor[: e.shape[0]] for e in expo]
        delta = rows_of([p * g for p, g in zip(probs, grads[h])], jnp.sum, jnp.add)
        moved = [p * (g - delta[: p.shape[0]]) for p, g in zip(probs, grads[h])]
        for values, store in ((probs, weights), (moved, steps)):
            store.append(
                [
                    regroup(values[0], MIXED_TO_SPLIT).astype(BF),
                    regroup(values[1], MIXED_TO_PAIR).astype(BF),
                    values[2].astype(BF),
                ]
            )

    for h in heads:
        for target, left, source, factor in (
            (attended, weights[h], value_lanes[h], None), (grad_query, steps[h], lanes[h], scale)
        ):
            r0 = jnp.concatenate([dot(left[0][b], split_ref[b, source]) for b in blocks], 0)
            r1 = jnp.concatenate([dot(left[1][b], pair_ref[b, source]) for b in pairs], 0)
            r2 = dot(left[2], far_rows[:, source])
            rows = grow(r2, regroup(r1, PAIR_TO_MIXED), jnp.add)
            rows = grow(rows, regroup(r0, SPLIT_TO_MIXED), jnp.add)
            target[:, lanes[h]] = rows if factor is None else rows * factor
        for left, right, target, factor in (
            (steps[h], (query_split_ref, query_pair_ref, query_ref), lanes[h], scale),
            (weights[h], (upstream_split_ref, upstream_pair_ref, upstream_ref), value_lanes[h], None),
        ):
            r0 = jnp.concatenate([dot_tn(left[0][b], right[0][b, lanes[h]]) for b in blocks], 0)
            r1 = jnp.concatenate([dot_tn(left[1][b], right[1][b, lanes[h]]) for b in pairs], 0)
            r2 = dot_tn(left[2], right[2][:, lanes[h]])
            rows = grow(r2[:TOK], regroup(r1, PAIR_TO_MIXED), jnp.add)
            rows = grow(rows, regroup(r0, SPLIT_TO_MIXED), jnp.add)
            near_ref[:, target] = rows if factor is None else rows * factor
            far_ref[:, target] = r2[TOK:] if factor is None else r2[TOK:] * factor

    wide[:, :32, :] = far_ref[TOK:, :].reshape(4, 32, 2 * PART)
    wide[:, 32:, :] = jnp.zeros((4, 32, 2 * PART), F32)
    wide[pl.ds(start, 2)] += far_ref[:TOK, :].reshape(2, 64, 2 * PART)
    around_out_ref[...] = wide[...].astype(BF)
    attended_ref[...] = swap_rows(attended[...]).astype(BF)
    grad_query_ref[...] = swap_rows(grad_query[...]).astype(BF)


def finish_kernel(
    attended_ref, valid_ref, order_ref, pick_ref, grad_out_ref, rows_ref, part_ref
):
    rows = jnp.where(valid_ref[...] > 0, dot_tn(order_ref[...], attended_ref[...]), 0.0).astype(BF)
    rows_ref[...] = rows
    part = dot_tn(rows, grad_out_ref[...]).astype(BF)
    for side in range(2):
        stacked = jnp.concatenate(
            [part[:, side * INNER + q * PART : side * INNER + (q + 1) * PART] for q in range(4)], 0
        )
        part_ref[side * INNER : (side + 1) * INNER, :] = dot_tn(pick_ref[...], stacked).astype(BF)


def value_kernel(near_ref, around_ref, order_ref, tokens_ref, out_part_ref, rows_ref, part_ref):
    rows = near_ref[...]
    rows = jnp.concatenate([rows[:64] + jnp.sum(around_ref[...].astype(F32), 0), rows[64:]], 0)
    rows = dot_tn(order_ref[...], swap_rows(rows).astype(BF)).astype(BF)
    rows_ref[...] = rows
    part_ref[:D, :] = dot_tn(tokens_ref[...], rows[:, PART:]).astype(BF)
    part_ref[D:, :] = out_part_ref[...]


def middle_kernel(pieces_ref, out_ref):
    yl = lax.axis_index("yl")
    sums = [jnp.sum(pieces_ref[:, member].astype(F32), 0) for member in range(4)]
    value = jnp.concatenate(sums, 1)
    other = [
        jnp.concatenate([part[q * 12 : (q + 1) * 12] for q in range(4)], 1) for part in sums
    ]
    rows = jnp.where(yl == 0, value, jnp.concatenate(other, 0))
    for index in range(16):
        out_ref[index] = rows[3 * index : 3 * index + 3].astype(BF)


def tokens_kernel(
    attended_ref, out_weight_ref, grad_query_ref, order_ref, rows_ref, columns_ref, pair_ref, rest_ref,
    kept_ref, sent_ref,
):
    pair = dot(columns_ref[...], pair_ref[...]).astype(BF)
    query = dot(columns_ref[...], rest_ref[:, :PART]).astype(BF)
    grad_query = dot_tn(order_ref[...], grad_query_ref[...]).astype(BF)
    mixed = dot(attended_ref[...], out_weight_ref[...])
    grads = dot_nt(grad_query, query) + dot_nt(rows_ref[...], pair)
    for index, rows in enumerate((mixed, grads)):
        for side in range(2):
            start = side * 2 * TOK
            kept_ref[side, index] = rows[start : start + TOK]
            sent_ref[side, index] = rows[start + TOK : start + 2 * TOK]


SCALARS = pl.BlockSpec(memory_space=pltpu.SMEM)
PAIR_WEIGHT = pl.BlockSpec((D, 2 * PART), lambda step: (0, 0))
REST_WEIGHT = pl.BlockSpec((D, 2 * PART), lambda step: (1, 0))


def call(kernel, shapes, *operands, scratch=(), flops=0, special={}, limit=VMEM_LIMIT):
    def whole(leaf):
        return pl.BlockSpec(leaf.shape, lambda step: (0,) * len(leaf.shape))

    specs = [special.get(index) or whole(leaf) for index, leaf in enumerate(operands)]
    return pl.pallas_call(
        kernel,
        grid=(1,),
        out_shape=shapes,
        in_specs=specs,
        out_specs=jax.tree.map(whole, shapes),
        scratch_shapes=list(scratch),
        compiler_params=pltpu.CompilerParams(vmem_limit_bytes=limit),
        cost_estimate=pl.CostEstimate(flops=flops, bytes_accessed=4_000_000, transcendentals=0),
    )(*operands)


def shape(*sizes, kind=BF):
    return jax.ShapeDtypeStruct(sizes, kind)


def reduce_weights(part, kept, sent):
    pieces = lax.all_to_all(part.reshape(32, 48, PART), PLANE, 0, 0, tiled=True).reshape(8, 4, 48, PART)
    pieces, sent = lax.optimization_barrier((pieces, sent))
    both = kept + partner(sent, "c")
    beside = partner(both[1].astype(BF), "yh")
    piece = call(middle_kernel, shape(16, 3, INNER), pieces, limit=8 * 1024 * 1024)
    piece = lax.all_to_all(piece, Z, 0, 0, tiled=True)
    piece = jnp.sum(piece.astype(F32), 0)
    full = lax.all_to_all(jnp.broadcast_to(piece[None], (8, 3, INNER)), SLIDE, 0, 0, tiled=True)
    value_share = full[:4].reshape(12, INNER)
    out_share = jnp.concatenate([full[4:6].reshape(6, INNER), full[6:].reshape(6, INNER)], 1)
    mixed = (both[0, 0] + beside[0].astype(F32)).astype(BF)
    grad_tokens = (both[0, 1] + beside[1].astype(F32)).astype(BF)
    return mixed, grad_tokens, value_share, out_share


def one_hot(source, size):
    return (jnp.arange(size, dtype=jnp.int32)[:, None] == source[None, :]).astype(BF)


def on_device(tokens, lengths, w_query, w_key, w_value, w_out, grad_out):
    length = lengths[0]
    core, yh = lax.axis_index("c"), lax.axis_index("yh")
    zh, zl = lax.axis_index("zh"), lax.axis_index("zl")
    block = ((zh * 4 + zl) * 2 + yh) * 2 + core
    turn = (yh * 2 + core) * 2

    mine = call(first_kernel, shape(16, 3, D), w_key, w_value, w_query, w_out)
    tokens, grad_out, mine = lax.optimization_barrier((tokens, grad_out, mine))
    own = jnp.concatenate([tokens[0], grad_out[0]], 0)
    other = partner(own, "yh")
    rows = lax.all_to_all(mine, Z, 0, 0, tiled=True)
    own, rows, length, turn, block, zl = lax.optimization_barrier((own, rows, length, turn, block, zl))
    chunks = call(
        chunk_kernel, shape(8, 4, 48, 2 * PART), rows, scratch=[pltpu.VMEM((48, D), F32)], limit=8 * 1024 * 1024
    )
    weights = lax.all_to_all(chunks.reshape(32, 48, 2 * PART), PLANE, 0, 0, tiled=True).reshape(2 * D, 2 * PART)

    both = jnp.concatenate([own, other], 0)
    both = jnp.stack([both, partner(both, "c")]).reshape(2, 2, 2, TOK, D)
    inputs = both[:, :, 0].transpose(1, 0, 2, 3).reshape(QUAD, D)
    upstream_rows = both[:, :, 1].transpose(1, 0, 2, 3).reshape(QUAD, D)

    row = jnp.arange(QUAD, dtype=jnp.int32)
    which = (row >> 3) & 3
    within = ((row & 7) << 4) + (reversed4(row >> 5) ^ turn)
    order = one_hot(which * TOK + within, QUAD).T
    valid = ((block ^ (row >> 7)) * TOK + (row & 127) < length).astype(F32)[:, None]

    column = jnp.arange(D, dtype=jnp.int32)
    spot, left = column // 48, column % 48
    columns = one_hot((left // 3 * 4 + (spot & 3)) * 12 + (spot >> 2) * 3 + left % 3, D)
    column = jnp.arange(INNER, dtype=jnp.int32)
    spot, left = column // 48, column % 48
    inner = (left % 12 // 3 * 4 + (spot & 3)) * 6 + (spot >> 2) * 3 + left % 3
    pick = one_hot(left // 12 * PART + inner, INNER)

    def key_position(member, size):
        return ((member ^ which[:size]) * TOK) + within[:size]

    base = ((row[:TOK] & 7) << 4) + (reversed4(row[:TOK] >> 3) ^ turn)
    pair_base = ((row[:TOK] & 7) << 4) + (reversed4(row[:TOK] >> 4) ^ turn)
    near_position = [(block ^ m) * TOK + base for m in range(4)]
    near_position += [((block ^ (p * 2)) ^ ((row[:TOK] >> 3) & 1)) * TOK + pair_base for p in range(2)]
    near_position = jnp.stack(near_position + near_position[:2])
    parts = [key_position(block, TOK)]
    start = (zl >> 1) * 2
    for index in range(2):
        parts.append(key_position(((zh * 4 + start + index) * 2 + yh) * 2 + core, 64))
    for index in range(4):
        parts.append(key_position(((zh * 4 + index) * 2 + yh) * 2 + core, 32))
    far_position = jnp.broadcast_to(jnp.concatenate(parts)[None], (8, FAR))
    limit = jnp.concatenate(
        [jnp.where(row[:TOK, None] < (QUAD >> scale), length, -1) + jnp.zeros((1, TOK), jnp.int32) for scale in (2, 3, 4)], 1
    )

    inputs_columns = dot(inputs, columns).astype(BF)
    tokens_rows = dot(order, inputs_columns).astype(BF)
    (
        upstream_rows, order, valid, columns, pick, near_position, far_position, limit, inputs_columns, tokens_rows,
    ) = lax.optimization_barrier(
        (upstream_rows, order, valid, columns, pick, near_position, far_position, limit, inputs_columns, tokens_rows)
    )

    rows_split, rows_pair, rows_near, sent = call(
        key_value_kernel,
        (shape(QUAD, 2 * PART), shape(2 * TOK, 2 * PART), shape(TOK, 2 * PART), shape(4, 64, 2 * PART)),
        tokens_rows, weights,
        special={1: PAIR_WEIGHT},
        limit=8 * 1024 * 1024,
        flops=200_000_000,
    )
    around = lax.all_to_all(sent, "zl", 0, 0, tiled=True)

    parted = (shape(QUAD, PART), shape(2 * TOK, PART), shape(TOK, PART))
    *queries, out_weight = call(
        query_kernel,
        parted + parted + (shape(PART, D),),
        tokens_rows, upstream_rows, valid, order, pick, weights,
        special={5: REST_WEIGHT},
        flops=3_000_000_000,
    )

    attended, grad_query, near_grads, around = call(
        attention_kernel,
        (shape(QUAD, PART), shape(QUAD, PART), shape(QUAD, 2 * PART, kind=F32), shape(4, 64, 2 * PART)),
        lengths, *queries, rows_split, rows_pair, rows_near, around, near_position, far_position, limit,
        scratch=[
            pltpu.VMEM((FAR, 2 * PART), BF), pltpu.VMEM((2 * TOK, 2 * PART), F32), pltpu.VMEM((4, 64, 2 * PART), F32),
            pltpu.VMEM((QUAD, PART), F32), pltpu.VMEM((QUAD, PART), F32),
        ],
        special={0: SCALARS},
        flops=3_000_000_000,
    )

    around = lax.all_to_all(around, "zl", 0, 0, tiled=True)
    attended, out_part = call(
        finish_kernel,
        (shape(QUAD, PART), shape(D, PART)),
        attended, valid, order, pick, upstream_rows,
        flops=3_000_000_000,
    )
    grad_rows, part = call(
        value_kernel,
        (shape(QUAD, 2 * PART), shape(2 * D, PART)),
        near_grads, around, order, inputs_columns, out_part,
        limit=8 * 1024 * 1024,
        flops=200_000_000,
    )
    kept, sent = call(
        tokens_kernel,
        (shape(2, 2, TOK, D, kind=F32), shape(2, 2, TOK, D, kind=F32)),
        attended, out_weight, grad_query, order, grad_rows, columns, weights, weights,
        special={6: PAIR_WEIGHT, 7: REST_WEIGHT},
        flops=3_000_000_000,
    )
    mixed, grad_tokens, value_share, out_share = reduce_weights(part, kept, sent)
    return mixed[None], grad_tokens[None], value_share, out_share


def solution(mesh):
    fine = Mesh(mesh.devices.reshape(2, 4, 4, 4, 2, 2), ("yl", "x", "zh", "zl", "yh", "c"))
    seq = ("zh", "zl", "yh", "c")
    rows = P(seq, None)
    whole = P(SLIDE, seq, None)
    return jax.shard_map(
        on_device,
        mesh=fine,
        in_specs=(whole, P(SLIDE), rows, rows, rows, rows, whole),
        out_specs=(whole, whole, rows, rows),
        check_vma=False,
    )
```

```python
import jax
import jax.numpy as jnp
from jax import lax
from jax.experimental import pallas as pl
from jax.experimental.pallas import tpu as pltpu
from jax.sharding import Mesh, PartitionSpec as P

D = 768
INNER = 384
TOK = 128
QUAD = 4 * TOK
DIM = 48
LOCAL_HEADS = 2
PART = LOCAL_HEADS * DIM
HALF = INNER // 2
STORED = QUAD + 3 * TOK
FAR = 3 * TOK
BF = jnp.bfloat16
F32 = jnp.float32
SLIDE = ("yl", "x")
Z = ("zh", "zl")
PLANE = ("yl", "x", "yh", "c")
VMEM_LIMIT = 24 * 1024 * 1024

SPLIT_TO_MIXED = [m * 128 + g * 8 for g in range(16) for m in range(4)]
MIXED_TO_SPLIT = [g * 32 + m * 8 for m in range(4) for g in range(16)]
PAIR_TO_MIXED = [(m >> 1) * 128 + g * 16 + (m & 1) * 8 for g in range(8) for m in range(4)]
MIXED_TO_PAIR = [g * 32 + (p * 2 + c) * 8 for p in range(2) for g in range(8) for c in range(2)]


def dot(a, b):
    return jnp.dot(a, b, preferred_element_type=F32)


def dot_nt(a, b):
    return lax.dot_general(a, b, (((1,), (1,)), ((), ())), preferred_element_type=F32)


def dot_tn(a, b):
    return lax.dot_general(a, b, (((0,), (0,)), ((), ())), preferred_element_type=F32)


def partner(value, axis):
    return lax.ppermute(value, axis, [(0, 1), (1, 0)])


def reversed4(value):
    return ((value & 1) << 3) | ((value & 2) << 1) | ((value & 4) >> 1) | ((value & 8) >> 3)


def regroup(rows, starts):
    return jnp.concatenate([rows[start : start + 8] for start in starts], 0)


def swap_rows(rows):
    lane = lax.broadcasted_iota(jnp.int32, rows.shape, 1)
    odd = (lane >= DIM) & (lane < 2 * DIM) | (lane >= 3 * DIM)
    moved = jnp.concatenate([rows[QUAD // 2 :], rows[: QUAD // 2]], 0)
    return jnp.where(odd, moved, rows)


def first_kernel(key_ref, value_ref, query_ref, out_weight_ref, out_ref):
    yl, x = lax.axis_index("yl"), lax.axis_index("x")
    query, key, value = (ref[...].astype(F32) for ref in (query_ref, key_ref, value_ref))
    out_weight = out_weight_ref[...].astype(F32)
    left = jnp.where(yl == 0, key, query)
    mine = None
    for index in range(4):
        rows = slice(3 * index, 3 * index + 3)
        out_rows = slice((index & 1) * 3, (index & 1) * 3 + 3)
        side = slice((index >> 1) * INNER, (index >> 1) * INNER + INNER)
        right = jnp.where(yl == 0, value[rows], out_weight[out_rows, side])
        part = jnp.concatenate([left[rows], right], 1)
        mine = part if mine is None else jnp.where(x == index, part, mine)
    out_ref[...] = jnp.broadcast_to(mine.astype(BF)[None], out_ref.shape)


def chunk_kernel(pieces_ref, out_ref, joined):
    yl = lax.axis_index("yl")
    for index in range(16):
        joined[3 * index : 3 * index + 3, :] = pieces_ref[index].astype(F32)
    rows = joined[...]
    for member in range(4):
        lanes = slice(member * PART, (member + 1) * PART)
        other = rows[member * 12 : (member + 1) * 12, INNER:]
        other = jnp.concatenate([other[:, q * PART : (q + 1) * PART] for q in range(4)], 0)
        right = jnp.where(yl == 0, rows[:, INNER:][:, lanes], other)
        chunk = jnp.concatenate([rows[:, lanes], right], 1)
        chunk = jnp.concatenate([chunk[:24], chunk[24:]], 1).astype(BF)
        for place in range(8):
            out_ref[place, member] = chunk


def project(rows, weight, lanes):
    low, high = slice(lanes.start, lanes.stop), slice(2 * PART + lanes.start, 2 * PART + lanes.stop)
    return dot(rows[:, :INNER], weight[:, low]) + dot(rows[:, INNER:], weight[:, high])


def store(out_ref, lanes, rows):
    out_ref[:QUAD, lanes] = regroup(rows, MIXED_TO_SPLIT).astype(BF)
    out_ref[QUAD : QUAD + 2 * TOK, lanes] = regroup(rows, MIXED_TO_PAIR).astype(BF)
    out_ref[QUAD + 2 * TOK :, lanes] = rows[:TOK].astype(BF)


def key_value_kernel(tokens_ref, weight_ref, out_ref, sent_ref):
    rows = swap_rows(project(tokens_ref[...], weight_ref[...], slice(0, 2 * PART)))
    store(out_ref, slice(0, 2 * PART), rows)
    for member in range(4):
        sent_ref[member] = rows[:64].astype(BF)


def query_kernel(tokens_ref, grad_out_ref, valid_ref, order_ref, pick_ref, rest_ref, rows_ref, out_ref):
    rest = rest_ref[...]
    query = swap_rows(project(tokens_ref[...], rest, slice(0, PART)))
    blocks = []
    for side in range(2):
        for lanes in (slice(PART, 2 * PART), slice(3 * PART, 4 * PART)):
            block = dot(pick_ref[...], rest[side * HALF : (side + 1) * HALF, lanes])
            blocks += [block[:PART], block[PART:]]
    out_weight = jnp.concatenate(blocks, 1).astype(BF)
    out_ref[...] = out_weight
    upstream = dot_nt(grad_out_ref[...], out_weight)
    upstream = jnp.where(valid_ref[...] > 0, upstream, 0.0).astype(BF)
    upstream = swap_rows(dot(order_ref[...], upstream))
    store(rows_ref, slice(0, 2 * PART), jnp.concatenate([query, upstream], 1))


def attention_kernel(
    length_ref, query_rows_ref, key_rows_ref, around_ref, position_ref,
    out_ref, near_ref, around_out_ref, far_rows, far_ref, wide, attended, grad_query,
):
    split, pair, near = slice(0, QUAD), slice(QUAD, QUAD + 2 * TOK), slice(QUAD + 2 * TOK, STORED)
    query_split_ref, query_pair_ref, query_ref = (query_rows_ref.at[rows] for rows in (split, pair, near))
    split_ref, pair_ref, rows_ref = (key_rows_ref.at[rows] for rows in (split, pair, near))
    scale = DIM ** -0.5
    length, start = length_ref[0], (lax.axis_index("zl") >> 1) * 2
    far_rows[:TOK, :] = rows_ref[...]
    far_rows[TOK : 2 * TOK, :] = around_ref[pl.ds(start, 2)].reshape(TOK, 2 * PART)
    far_rows[2 * TOK :, :] = around_ref[:, :32, :].reshape(TOK, 2 * PART)
    place = lax.broadcasted_iota(jnp.int32, (TOK, FAR), 0)
    lane = lax.broadcasted_iota(jnp.int32, (TOK, FAR), 1)
    used = jnp.where(lane < TOK, TOK, jnp.where(lane < 2 * TOK, TOK // 2, TOK // 4))
    limit = jnp.where(place < used, length, -1)
    heads = range(LOCAL_HEADS)
    lanes = [slice(h * DIM, (h + 1) * DIM) for h in heads]
    value_lanes = [slice(PART + h * DIM, PART + (h + 1) * DIM) for h in heads]
    blocks = [slice(m * TOK, (m + 1) * TOK) for m in range(4)]
    pairs = blocks[:2]

    def grow(low, high, combine):
        size = low.shape[0]
        return jnp.concatenate([combine(high[:size], low), high[size:]], 0)

    scores, grads = [], []
    for h in heads:
        def masked(query, keys, position):
            position = position ^ h
            return jnp.where(position < length, dot_nt(query, keys) * scale, jnp.float32(-1e9))

        s0 = [masked(query_split_ref[b, lanes[h]], split_ref[b, lanes[h]], position_ref[m : m + 1, :TOK]) for m, b in enumerate(blocks)]
        s1 = [masked(query_pair_ref[b, lanes[h]], pair_ref[b, lanes[h]], position_ref[4 + p : 5 + p, :TOK]) for p, b in enumerate(pairs)]
        s2 = dot_nt(query_ref[:, lanes[h]], far_rows[:, lanes[h]]) * scale
        position = jnp.broadcast_to(position_ref[:1, TOK:] ^ h, s2.shape)
        s2 = jnp.where(position < limit, s2, jnp.float32(-1e9))
        scores.append(
            [regroup(jnp.concatenate(s0, 0), SPLIT_TO_MIXED), regroup(jnp.concatenate(s1, 0), PAIR_TO_MIXED), s2]
        )
    for h in heads:
        g0 = [dot_nt(query_split_ref[b, value_lanes[h]], split_ref[b, value_lanes[h]]) for b in blocks]
        g1 = [dot_nt(query_pair_ref[b, value_lanes[h]], pair_ref[b, value_lanes[h]]) for b in pairs]
        g2 = dot_nt(query_ref[:, value_lanes[h]], far_rows[:, value_lanes[h]])
        grads.append(
            [regroup(jnp.concatenate(g0, 0), SPLIT_TO_MIXED), regroup(jnp.concatenate(g1, 0), PAIR_TO_MIXED), g2]
        )

    weights, steps = [], []
    for h in heads:
        def rows_of(values, reduce, combine):
            total = reduce(values[2], axis=1, keepdims=True)
            for value in (values[1], values[0]):
                total = grow(total, reduce(value, axis=1, keepdims=True), combine)
            return total

        top = rows_of(scores[h], jnp.max, jnp.maximum)
        expo = [jnp.exp(s - top[: s.shape[0]]) for s in scores[h]]
        factor = 1.0 / rows_of(expo, jnp.sum, jnp.add)
        probs = [e * factor[: e.shape[0]] for e in expo]
        delta = rows_of([p * g for p, g in zip(probs, grads[h])], jnp.sum, jnp.add)
        moved = [p * (g - delta[: p.shape[0]]) for p, g in zip(probs, grads[h])]
        for values, store in ((probs, weights), (moved, steps)):
            store.append(
                [
                    regroup(values[0], MIXED_TO_SPLIT).astype(BF),
                    regroup(values[1], MIXED_TO_PAIR).astype(BF),
                    values[2].astype(BF),
                ]
            )

    for h in heads:
        for target, left, source, factor in (
            (attended, weights[h], value_lanes[h], None), (grad_query, steps[h], lanes[h], scale)
        ):
            r0 = jnp.concatenate([dot(left[0][b], split_ref[b, source]) for b in blocks], 0)
            r1 = jnp.concatenate([dot(left[1][b], pair_ref[b, source]) for b in pairs], 0)
            r2 = dot(left[2], far_rows[:, source])
            rows = grow(r2, regroup(r1, PAIR_TO_MIXED), jnp.add)
            rows = grow(rows, regroup(r0, SPLIT_TO_MIXED), jnp.add)
            target[:, lanes[h]] = rows if factor is None else rows * factor
        for left, right, target, factor in (
            (steps[h], (query_split_ref, query_pair_ref, query_ref), lanes[h], scale),
            (weights[h], (query_split_ref, query_pair_ref, query_ref), value_lanes[h], None),
        ):
            r0 = jnp.concatenate([dot_tn(left[0][b], right[0][b, target]) for b in blocks], 0)
            r1 = jnp.concatenate([dot_tn(left[1][b], right[1][b, target]) for b in pairs], 0)
            r2 = dot_tn(left[2], right[2][:, target])
            rows = grow(r2[:TOK], regroup(r1, PAIR_TO_MIXED), jnp.add)
            rows = grow(rows, regroup(r0, SPLIT_TO_MIXED), jnp.add)
            near_ref[:, target] = rows if factor is None else rows * factor
            far_ref[:, target] = r2[TOK:] if factor is None else r2[TOK:] * factor

    wide[:, :32, :] = far_ref[TOK:, :].reshape(4, 32, 2 * PART)
    wide[:, 32:, :] = jnp.zeros((4, 32, 2 * PART), F32)
    wide[pl.ds(start, 2)] += far_ref[:TOK, :].reshape(2, 64, 2 * PART)
    around_out_ref[...] = wide[...].astype(BF)
    rows = jnp.concatenate([attended[...], grad_query[...]], 1)
    out_ref[...] = swap_rows(rows).astype(BF)


def finish_kernel(
    attended_ref, valid_ref, order_ref, pick_ref, grad_out_ref, rows_ref, part_ref
):
    rows = jnp.where(valid_ref[...] > 0, dot_tn(order_ref[...], attended_ref[:, :PART]), 0.0).astype(BF)
    rows_ref[...] = rows
    part = dot_tn(rows, grad_out_ref[...]).astype(BF)
    for side in range(2):
        for high in range(2):
            start = side * INNER + high * 2 * PART
            stacked = jnp.concatenate([part[:, start : start + PART], part[:, start + PART : start + 2 * PART]], 0)
            part_ref[side * HALF : (side + 1) * HALF, high * PART : (high + 1) * PART] = dot_tn(
                pick_ref[...], stacked
            ).astype(BF)


def value_kernel(near_ref, around_ref, tokens_ref, out_part_ref, rows_ref, part_ref):
    rows = near_ref[...]
    rows = jnp.concatenate([rows[:64] + jnp.sum(around_ref[...].astype(F32), 0), rows[64:]], 0)
    rows = swap_rows(rows).astype(BF)
    rows_ref[...] = rows
    part_ref[:INNER, :PART] = dot_tn(tokens_ref[:, :INNER], rows[:, PART:]).astype(BF)
    part_ref[:INNER, PART:] = dot_tn(tokens_ref[:, INNER:], rows[:, PART:]).astype(BF)
    part_ref[INNER:, :] = out_part_ref[...]


def middle_kernel(pieces_ref, out_ref):
    yl = lax.axis_index("yl")
    sums = [jnp.sum(pieces_ref[:, member].astype(F32), 0) for member in range(4)]
    halves = slice(0, PART), slice(PART, 2 * PART)
    value = [jnp.concatenate([part[:, lanes] for part in sums], 1) for lanes in halves]
    other = [
        jnp.concatenate([part[rows, lanes] for lanes in halves for rows in (slice(0, 12), slice(12, 24))], 1)
        for part in sums
    ]
    rows = jnp.where(yl == 0, jnp.concatenate(value, 0), jnp.concatenate(other, 0))
    for index in range(16):
        out_ref[index] = rows[3 * index : 3 * index + 3].astype(BF)


def tokens_kernel(
    attended_ref, out_weight_ref, grad_query_ref, order_ref, rows_ref, columns_ref, pair_ref, rest_ref,
    kept_ref, sent_ref,
):
    pair = project(columns_ref[...], pair_ref[...], slice(0, 2 * PART)).astype(BF)
    query = project(columns_ref[...], rest_ref[...], slice(0, PART)).astype(BF)
    order = order_ref[...]
    grad_query = dot_tn(order, grad_query_ref[:, PART:]).astype(BF)
    grad_rows = dot_tn(order, rows_ref[...]).astype(BF)
    mixed = dot(attended_ref[...], out_weight_ref[...])
    grads = dot_nt(grad_query, query) + dot_nt(grad_rows, pair)
    for index, rows in enumerate((mixed, grads)):
        for side in range(2):
            start = side * 2 * TOK
            kept_ref[side, index] = rows[start : start + TOK]
            sent_ref[side, index] = rows[start + TOK : start + 2 * TOK]


SCALARS = pl.BlockSpec(memory_space=pltpu.SMEM)
PAIR_WEIGHT = pl.BlockSpec((INNER, 4 * PART), lambda step: (0, 0))
REST_WEIGHT = pl.BlockSpec((INNER, 4 * PART), lambda step: (1, 0))


def call(kernel, shapes, *operands, scratch=(), flops=0, special={}, near=(), loose=()):
    def whole(leaf):
        return pl.BlockSpec(leaf.shape, lambda step: (0,) * len(leaf.shape))

    specs = [special.get(index) or whole(leaf) for index, leaf in enumerate(operands)]
    operands = [
        leaf if index in near or special.get(index) is SCALARS else pltpu.with_memory_space_constraint(leaf, pltpu.HBM)
        for index, leaf in enumerate(operands)
    ]
    return pl.pallas_call(
        kernel,
        grid=(1,),
        out_shape=[
            leaf if index in loose else pltpu.HBM(leaf.shape, leaf.dtype) for index, leaf in enumerate(shapes)
        ],
        in_specs=specs,
        out_specs=[whole(leaf) for leaf in shapes],
        scratch_shapes=list(scratch),
        compiler_params=pltpu.CompilerParams(vmem_limit_bytes=VMEM_LIMIT),
        cost_estimate=pl.CostEstimate(flops=flops, bytes_accessed=4_000_000, transcendentals=0),
    )(*operands)


def shape(*sizes, kind=BF):
    return jax.ShapeDtypeStruct(sizes, kind)


def reduce_weights(part, kept, sent):
    pieces = lax.all_to_all(part.reshape(32, 24, 2 * PART), PLANE, 0, 0, tiled=True).reshape(8, 4, 24, 2 * PART)
    pieces, sent = lax.optimization_barrier((pieces, sent))
    both = kept + partner(sent, "c")
    beside = partner(both[1].astype(BF), "yh")
    (piece,) = call(middle_kernel, [shape(16, 3, INNER)], pieces, near=(0,), loose=(0,))
    piece = lax.all_to_all(piece, Z, 0, 0, tiled=True)
    piece = jnp.sum(piece.astype(F32), 0)
    full = lax.all_to_all(jnp.broadcast_to(piece[None], (8, 3, INNER)), SLIDE, 0, 0, tiled=True)
    value_share = full[:4].reshape(12, INNER)
    out_share = jnp.concatenate([full[4:6].reshape(6, INNER), full[6:].reshape(6, INNER)], 1)
    mixed = (both[0, 0] + beside[0].astype(F32)).astype(BF)
    grad_tokens = (both[0, 1] + beside[1].astype(F32)).astype(BF)
    return mixed, grad_tokens, value_share, out_share


def one_hot(source, size):
    return (jnp.arange(size, dtype=jnp.int32)[:, None] == source[None, :]).astype(BF)


def on_device(tokens, lengths, w_query, w_key, w_value, w_out, grad_out):
    length = lengths[0]
    core, yh = lax.axis_index("c"), lax.axis_index("yh")
    zh, zl = lax.axis_index("zh"), lax.axis_index("zl")
    block = ((zh * 4 + zl) * 2 + yh) * 2 + core
    turn = (yh * 2 + core) * 2

    (mine,) = call(first_kernel, [shape(16, 3, D)], w_key, w_value, w_query, w_out, loose=(0,))
    tokens, grad_out, mine = lax.optimization_barrier((tokens, grad_out, mine))
    own = jnp.concatenate([tokens[0], grad_out[0]], 0)
    other = partner(own, "yh")
    rows = lax.all_to_all(mine, Z, 0, 0, tiled=True)
    own, rows, length, turn, block, zl = lax.optimization_barrier((own, rows, length, turn, block, zl))
    (chunks,) = call(
        chunk_kernel, [shape(8, 4, 24, 4 * PART)], rows, scratch=[pltpu.VMEM((48, D), F32)], near=(0,), loose=(0,)
    )
    weights = lax.all_to_all(chunks.reshape(32, 24, 4 * PART), PLANE, 0, 0, tiled=True).reshape(D, 4 * PART)

    both = jnp.concatenate([own, other], 0)
    both = jnp.stack([both, partner(both, "c")]).reshape(2, 2, 2, TOK, D)
    inputs = both[:, :, 0].transpose(1, 0, 2, 3).reshape(QUAD, D)
    upstream_rows = both[:, :, 1].transpose(1, 0, 2, 3).reshape(QUAD, D)

    row = jnp.arange(QUAD, dtype=jnp.int32)
    which = (row >> 3) & 3
    within = ((row & 7) << 4) + (reversed4(row >> 5) ^ turn)
    order = one_hot(which * TOK + within, QUAD).T
    valid = ((block ^ (row >> 7)) * TOK + (row & 127) < length).astype(F32)[:, None]

    column = jnp.arange(D, dtype=jnp.int32)
    high, spot, left = column // INNER, column % INNER // 24, column % 24
    columns = one_hot(((high * 8 + left // 3) * 4 + (spot & 3)) * 12 + (spot >> 2) * 3 + left % 3, D)
    column = jnp.arange(HALF, dtype=jnp.int32)
    spot, left = column // 24, column % 24
    inner = (left % 12 // 3 * 4 + (spot & 3)) * 6 + (spot >> 2) * 3 + left % 3
    pick = one_hot(left // 12 * PART + inner, HALF)

    def key_position(member, size):
        return ((member ^ which[:size]) * TOK) + within[:size]

    base = ((row[:TOK] & 7) << 4) + (reversed4(row[:TOK] >> 3) ^ turn)
    pair_base = ((row[:TOK] & 7) << 4) + (reversed4(row[:TOK] >> 4) ^ turn)
    near_position = [(block ^ m) * TOK + base for m in range(4)]
    near_position += [((block ^ (p * 2)) ^ ((row[:TOK] >> 3) & 1)) * TOK + pair_base for p in range(2)]
    near_position = jnp.stack(near_position + near_position[:2])
    parts = [key_position(block, TOK)]
    start = (zl >> 1) * 2
    for index in range(2):
        parts.append(key_position(((zh * 4 + start + index) * 2 + yh) * 2 + core, 64))
    for index in range(4):
        parts.append(key_position(((zh * 4 + index) * 2 + yh) * 2 + core, 32))
    far_position = jnp.broadcast_to(jnp.concatenate(parts)[None], (8, FAR))
    position = jnp.concatenate([near_position, far_position], 1)

    tokens_rows = dot(order, dot(inputs, columns).astype(BF)).astype(BF)
    (
        upstream_rows, order, valid, columns, pick, position, tokens_rows,
    ) = lax.optimization_barrier(
        (upstream_rows, order, valid, columns, pick, position, tokens_rows)
    )

    key_rows, sent = call(
        key_value_kernel,
        (shape(STORED, 2 * PART), shape(4, 64, 2 * PART)),
        tokens_rows, weights,
        special={1: PAIR_WEIGHT},
        near=(0, 1),
        loose=(1,),
        flops=200_000_000,
    )
    around = lax.all_to_all(sent, "zl", 0, 0, tiled=True)
    query_rows, out_weight = call(
        query_kernel,
        (shape(STORED, 2 * PART), shape(PART, D)),
        tokens_rows, upstream_rows, valid, order, pick, weights,
        special={5: REST_WEIGHT},
        flops=3_000_000_000,
    )

    both, near_grads, around = call(
        attention_kernel,
        (shape(QUAD, 2 * PART), shape(QUAD, 2 * PART, kind=F32), shape(4, 64, 2 * PART)),
        lengths, query_rows, key_rows, around, position,
        scratch=[
            pltpu.VMEM((FAR, 2 * PART), BF), pltpu.VMEM((2 * TOK, 2 * PART), F32), pltpu.VMEM((4, 64, 2 * PART), F32),
            pltpu.VMEM((QUAD, PART), F32), pltpu.VMEM((QUAD, PART), F32),
        ],
        special={0: SCALARS},
        near=(3,),
        loose=(2,),
        flops=3_000_000_000,
    )

    around = lax.all_to_all(around, "zl", 0, 0, tiled=True)
    attended, out_part = call(
        finish_kernel,
        (shape(QUAD, PART), shape(INNER, 2 * PART)),
        both, valid, order, pick, upstream_rows,
        flops=3_000_000_000,
    )
    grad_rows, part = call(
        value_kernel,
        (shape(QUAD, 2 * PART), shape(D, 2 * PART)),
        near_grads, around, tokens_rows, out_part,
        near=(1,),
        loose=(1,),
        flops=200_000_000,
    )
    kept, sent = call(
        tokens_kernel,
        (shape(2, 2, TOK, D, kind=F32), shape(2, 2, TOK, D, kind=F32)),
        attended, out_weight, both, order, grad_rows, columns, weights, weights,
        special={6: PAIR_WEIGHT, 7: REST_WEIGHT},
        flops=3_000_000_000,
    )
    mixed, grad_tokens, value_share, out_share = reduce_weights(part, kept, sent)
    return mixed[None], grad_tokens[None], value_share, out_share


def solution(mesh):
    fine = Mesh(mesh.devices.reshape(2, 4, 4, 4, 2, 2), ("yl", "x", "zh", "zl", "yh", "c"))
    seq = ("zh", "zl", "yh", "c")
    rows = P(seq, None)
    whole = P(SLIDE, seq, None)
    return jax.shard_map(
        on_device,
        mesh=fine,
        in_specs=(whole, P(SLIDE), rows, rows, rows, rows, whole),
        out_specs=(whole, whole, rows, rows),
        check_vma=False,
    )
```

```python
import jax
import jax.numpy as jnp
from jax import lax
from jax.experimental import pallas as pl
from jax.experimental.pallas import tpu as pltpu
from jax.sharding import Mesh, PartitionSpec as P

D = 768
INNER = 384
TOK = 128
QUAD = 4 * TOK
DIM = 48
LOCAL_HEADS = 2
PART = LOCAL_HEADS * DIM
HALF = INNER // 2
STORED = QUAD + 3 * TOK
FAR = 3 * TOK
BF = jnp.bfloat16
F32 = jnp.float32
SLIDE = ("yl", "x")
Z = ("zh", "zl")
PLANE = ("yl", "x", "yh", "c")
VMEM_LIMIT = 24 * 1024 * 1024

SPLIT_TO_MIXED = [m * 128 + g * 8 for g in range(16) for m in range(4)]
MIXED_TO_SPLIT = [g * 32 + m * 8 for m in range(4) for g in range(16)]
PAIR_TO_MIXED = [(m >> 1) * 128 + g * 16 + (m & 1) * 8 for g in range(8) for m in range(4)]
MIXED_TO_PAIR = [g * 32 + (p * 2 + c) * 8 for p in range(2) for g in range(8) for c in range(2)]


def dot(a, b):
    return jnp.dot(a, b, preferred_element_type=F32)


def dot_nt(a, b):
    return lax.dot_general(a, b, (((1,), (1,)), ((), ())), preferred_element_type=F32)


def dot_tn(a, b):
    return lax.dot_general(a, b, (((0,), (0,)), ((), ())), preferred_element_type=F32)


def partner(value, axis):
    return lax.ppermute(value, axis, [(0, 1), (1, 0)])


def reversed4(value):
    return ((value & 1) << 3) | ((value & 2) << 1) | ((value & 4) >> 1) | ((value & 8) >> 3)


def regroup(rows, starts):
    return jnp.concatenate([rows[start : start + 8] for start in starts], 0)


def swap_rows(rows):
    lane = lax.broadcasted_iota(jnp.int32, rows.shape, 1)
    odd = (lane >= DIM) & (lane < 2 * DIM) | (lane >= 3 * DIM)
    moved = jnp.concatenate([rows[QUAD // 2 :], rows[: QUAD // 2]], 0)
    return jnp.where(odd, moved, rows)


def first_kernel(key_ref, value_ref, query_ref, out_weight_ref, out_ref):
    yl, x = lax.axis_index("yl"), lax.axis_index("x")
    query, key, value = (ref[...].astype(F32) for ref in (query_ref, key_ref, value_ref))
    out_weight = out_weight_ref[...].astype(F32)
    left = jnp.where(yl == 0, key, query)
    mine = None
    for index in range(4):
        rows = slice(3 * index, 3 * index + 3)
        out_rows = slice((index & 1) * 3, (index & 1) * 3 + 3)
        side = slice((index >> 1) * INNER, (index >> 1) * INNER + INNER)
        right = jnp.where(yl == 0, value[rows], out_weight[out_rows, side])
        part = jnp.concatenate([left[rows], right], 1)
        mine = part if mine is None else jnp.where(x == index, part, mine)
    out_ref[...] = jnp.broadcast_to(mine.astype(BF)[None], out_ref.shape)


def chunk_kernel(pieces_ref, out_ref, joined):
    yl = lax.axis_index("yl")
    for index in range(16):
        joined[3 * index : 3 * index + 3, :] = pieces_ref[index].astype(F32)
    rows = joined[...]
    for member in range(4):
        lanes = slice(member * PART, (member + 1) * PART)
        other = rows[member * 12 : (member + 1) * 12, INNER:]
        other = jnp.concatenate([other[:, q * PART : (q + 1) * PART] for q in range(4)], 0)
        right = jnp.where(yl == 0, rows[:, INNER:][:, lanes], other)
        chunk = jnp.concatenate([rows[:, lanes], right], 1)
        chunk = jnp.concatenate([chunk[:24], chunk[24:]], 1).astype(BF)
        for place in range(8):
            out_ref[place, member] = chunk


def project(rows, weight, lanes):
    low, high = slice(lanes.start, lanes.stop), slice(2 * PART + lanes.start, 2 * PART + lanes.stop)
    return dot(rows[:, :INNER], weight[:, low]) + dot(rows[:, INNER:], weight[:, high])


def store(out_ref, lanes, rows):
    out_ref[:QUAD, lanes] = regroup(rows, MIXED_TO_SPLIT).astype(BF)
    out_ref[QUAD : QUAD + 2 * TOK, lanes] = regroup(rows, MIXED_TO_PAIR).astype(BF)
    out_ref[QUAD + 2 * TOK :, lanes] = rows[:TOK].astype(BF)


def sent_kernel(even_ref, odd_ref, weight_ref, out_ref):
    weight = weight_ref[...]
    even, odd = (project(ref[...], weight, slice(0, 2 * PART)) for ref in (even_ref, odd_ref))
    lane = lax.broadcasted_iota(jnp.int32, even.shape, 1)
    rows = jnp.where((lane >= DIM) & (lane < 2 * DIM) | (lane >= 3 * DIM), odd, even).astype(BF)
    for member in range(4):
        out_ref[member] = rows


def query_kernel(
    tokens_ref, grad_out_ref, valid_ref, order_ref, pick_ref, pair_ref, rest_ref, rows_ref, key_rows_ref, out_ref
):
    lanes = slice(0, 2 * PART)
    store(key_rows_ref, lanes, swap_rows(project(tokens_ref[...], pair_ref[...], lanes)))
    rest = rest_ref[...]
    query = swap_rows(project(tokens_ref[...], rest, slice(0, PART)))
    blocks = []
    for side in range(2):
        for lanes in (slice(PART, 2 * PART), slice(3 * PART, 4 * PART)):
            block = dot(pick_ref[...], rest[side * HALF : (side + 1) * HALF, lanes])
            blocks += [block[:PART], block[PART:]]
    out_weight = jnp.concatenate(blocks, 1).astype(BF)
    out_ref[...] = out_weight
    upstream = dot_nt(grad_out_ref[...], out_weight)
    upstream = jnp.where(valid_ref[...] > 0, upstream, 0.0).astype(BF)
    upstream = swap_rows(dot(order_ref[...], upstream))
    store(rows_ref, slice(0, 2 * PART), jnp.concatenate([query, upstream], 1))


def attention_kernel(
    length_ref, query_rows_ref, key_rows_ref, around_ref, position_ref,
    out_ref, near_ref, around_out_ref, far_rows, far_ref, wide, attended, grad_query,
):
    split, pair, near = slice(0, QUAD), slice(QUAD, QUAD + 2 * TOK), slice(QUAD + 2 * TOK, STORED)
    query_split_ref, query_pair_ref, query_ref = (query_rows_ref.at[rows] for rows in (split, pair, near))
    split_ref, pair_ref, rows_ref = (key_rows_ref.at[rows] for rows in (split, pair, near))
    scale = DIM ** -0.5
    length, start = length_ref[0], (lax.axis_index("zl") >> 1) * 2
    far_rows[:TOK, :] = rows_ref[...]
    far_rows[TOK : 2 * TOK, :] = around_ref[pl.ds(start, 2)].reshape(TOK, 2 * PART)
    far_rows[2 * TOK :, :] = around_ref[:, :32, :].reshape(TOK, 2 * PART)
    place = lax.broadcasted_iota(jnp.int32, (TOK, FAR), 0)
    lane = lax.broadcasted_iota(jnp.int32, (TOK, FAR), 1)
    used = jnp.where(lane < TOK, TOK, jnp.where(lane < 2 * TOK, TOK // 2, TOK // 4))
    limit = jnp.where(place < used, length, -1)
    heads = range(LOCAL_HEADS)
    lanes = [slice(h * DIM, (h + 1) * DIM) for h in heads]
    value_lanes = [slice(PART + h * DIM, PART + (h + 1) * DIM) for h in heads]
    blocks = [slice(m * TOK, (m + 1) * TOK) for m in range(4)]
    pairs = blocks[:2]

    def grow(low, high, combine):
        size = low.shape[0]
        return jnp.concatenate([combine(high[:size], low), high[size:]], 0)

    scores, grads = [], []
    for h in heads:
        def masked(query, keys, position):
            position = position ^ h
            return jnp.where(position < length, dot_nt(query, keys) * scale, jnp.float32(-1e9))

        s0 = [masked(query_split_ref[b, lanes[h]], split_ref[b, lanes[h]], position_ref[m : m + 1, :TOK]) for m, b in enumerate(blocks)]
        s1 = [masked(query_pair_ref[b, lanes[h]], pair_ref[b, lanes[h]], position_ref[4 + p : 5 + p, :TOK]) for p, b in enumerate(pairs)]
        s2 = dot_nt(query_ref[:, lanes[h]], far_rows[:, lanes[h]]) * scale
        position = jnp.broadcast_to(position_ref[:1, TOK:] ^ h, s2.shape)
        s2 = jnp.where(position < limit, s2, jnp.float32(-1e9))
        scores.append(
            [regroup(jnp.concatenate(s0, 0), SPLIT_TO_MIXED), regroup(jnp.concatenate(s1, 0), PAIR_TO_MIXED), s2]
        )
    for h in heads:
        g0 = [dot_nt(query_split_ref[b, value_lanes[h]], split_ref[b, value_lanes[h]]) for b in blocks]
        g1 = [dot_nt(query_pair_ref[b, value_lanes[h]], pair_ref[b, value_lanes[h]]) for b in pairs]
        g2 = dot_nt(query_ref[:, value_lanes[h]], far_rows[:, value_lanes[h]])
        grads.append(
            [regroup(jnp.concatenate(g0, 0), SPLIT_TO_MIXED), regroup(jnp.concatenate(g1, 0), PAIR_TO_MIXED), g2]
        )

    weights, steps = [], []
    for h in heads:
        def rows_of(values, reduce, combine):
            total = combine(combine(values[2][:, :TOK], values[2][:, TOK : 2 * TOK]), values[2][:, 2 * TOK :])
            total = grow(grow(total, values[1], combine), values[0], combine)
            return reduce(total, axis=1, keepdims=True)

        top = rows_of(scores[h], jnp.max, jnp.maximum)
        expo = [jnp.exp(s - top[: s.shape[0]]) for s in scores[h]]
        factor = 1.0 / rows_of(expo, jnp.sum, jnp.add)
        probs = [e * factor[: e.shape[0]] for e in expo]
        delta = rows_of([p * g for p, g in zip(probs, grads[h])], jnp.sum, jnp.add)
        moved = [p * (g - delta[: p.shape[0]]) for p, g in zip(probs, grads[h])]
        for values, store in ((probs, weights), (moved, steps)):
            store.append(
                [
                    regroup(values[0], MIXED_TO_SPLIT).astype(BF),
                    regroup(values[1], MIXED_TO_PAIR).astype(BF),
                    values[2].astype(BF),
                ]
            )

    for h in heads:
        for target, left, source, factor in (
            (attended, weights[h], value_lanes[h], None), (grad_query, steps[h], lanes[h], scale)
        ):
            r0 = jnp.concatenate([dot(left[0][b], split_ref[b, source]) for b in blocks], 0)
            r1 = jnp.concatenate([dot(left[1][b], pair_ref[b, source]) for b in pairs], 0)
            r2 = dot(left[2], far_rows[:, source])
            rows = grow(r2, regroup(r1, PAIR_TO_MIXED), jnp.add)
            rows = grow(rows, regroup(r0, SPLIT_TO_MIXED), jnp.add)
            target[:, lanes[h]] = rows if factor is None else rows * factor
        for left, right, target, factor in (
            (steps[h], (query_split_ref, query_pair_ref, query_ref), lanes[h], scale),
            (weights[h], (query_split_ref, query_pair_ref, query_ref), value_lanes[h], None),
        ):
            r0 = jnp.concatenate([dot_tn(left[0][b], right[0][b, target]) for b in blocks], 0)
            r1 = jnp.concatenate([dot_tn(left[1][b], right[1][b, target]) for b in pairs], 0)
            r2 = dot_tn(left[2], right[2][:, target])
            rows = grow(r2[:TOK], regroup(r1, PAIR_TO_MIXED), jnp.add)
            rows = grow(rows, regroup(r0, SPLIT_TO_MIXED), jnp.add)
            near_ref[:, target] = rows if factor is None else rows * factor
            far_ref[:, target] = r2[TOK:] if factor is None else r2[TOK:] * factor

    wide[:, :32, :] = far_ref[TOK:, :].reshape(4, 32, 2 * PART)
    wide[:, 32:, :] = jnp.zeros((4, 32, 2 * PART), F32)
    wide[pl.ds(start, 2)] += far_ref[:TOK, :].reshape(2, 64, 2 * PART)
    around_out_ref[...] = wide[...].astype(BF)
    rows = jnp.concatenate([attended[...], grad_query[...]], 1)
    out_ref[...] = swap_rows(rows).astype(BF)


def finish_kernel(
    attended_ref, valid_ref, order_ref, pick_ref, grad_out_ref, rows_ref, part_ref
):
    rows = jnp.where(valid_ref[...] > 0, dot_tn(order_ref[...], attended_ref[:, :PART]), 0.0).astype(BF)
    rows_ref[...] = rows
    part = dot_tn(rows, grad_out_ref[...]).astype(BF)
    for side in range(2):
        for high in range(2):
            start = side * INNER + high * 2 * PART
            stacked = jnp.concatenate([part[:, start : start + PART], part[:, start + PART : start + 2 * PART]], 0)
            part_ref[side * HALF : (side + 1) * HALF, high * PART : (high + 1) * PART] = dot_tn(
                pick_ref[...], stacked
            ).astype(BF)


def key_value_grads(near_ref, around_ref):
    rows = near_ref[...]
    rows = jnp.concatenate([rows[:64] + jnp.sum(around_ref[...].astype(F32), 0), rows[64:]], 0)
    return swap_rows(rows).astype(BF)


def value_kernel(near_ref, around_ref, tokens_ref, out_part_ref, part_ref):
    rows = key_value_grads(near_ref, around_ref)
    part = dot_tn(rows[:, PART:], tokens_ref[...])
    part_ref[:INNER, :PART] = part[:, :INNER].T.astype(BF)
    part_ref[:INNER, PART:] = part[:, INNER:].T.astype(BF)
    part_ref[INNER:, :] = out_part_ref[...]


def middle_kernel(pieces_ref, out_ref):
    yl = lax.axis_index("yl")
    sums = [jnp.sum(pieces_ref[:, member].astype(F32), 0) for member in range(4)]
    halves = slice(0, PART), slice(PART, 2 * PART)
    value = [jnp.concatenate([part[:, lanes] for part in sums], 1) for lanes in halves]
    other = [
        jnp.concatenate([part[rows, lanes] for lanes in halves for rows in (slice(0, 12), slice(12, 24))], 1)
        for part in sums
    ]
    rows = jnp.where(yl == 0, jnp.concatenate(value, 0), jnp.concatenate(other, 0))
    for index in range(16):
        out_ref[index] = rows[3 * index : 3 * index + 3].astype(BF)


def last_kernel(pieces_ref, value_ref, out_ref):
    for x in range(4):
        value_ref[3 * x : 3 * x + 3, :] = pieces_ref[x]
        rows, side = (x & 1) * 3, (x >> 1) * INNER
        out_ref[rows : rows + 3, side : side + INNER] = pieces_ref[4 + x]


def tokens_kernel(
    attended_ref, out_weight_ref, grad_query_ref, order_ref, near_ref, around_ref, columns_ref, pair_ref, rest_ref,
    kept_ref, sent_ref,
):
    pair = project(columns_ref[...], pair_ref[...], slice(0, 2 * PART)).astype(BF)
    query = project(columns_ref[...], rest_ref[...], slice(0, PART)).astype(BF)
    order = order_ref[...]
    grad_query = dot_tn(order, grad_query_ref[:, PART:]).astype(BF)
    grad_rows = dot_tn(order, key_value_grads(near_ref, around_ref)).astype(BF)
    mixed = dot(attended_ref[...], out_weight_ref[...])
    grads = dot_nt(grad_query, query) + dot_nt(grad_rows, pair)
    for index, rows in enumerate((mixed, grads)):
        for side in range(2):
            start = side * 2 * TOK
            kept_ref[side, index] = rows[start : start + TOK]
            sent_ref[side, index] = rows[start + TOK : start + 2 * TOK]


SCALARS = pl.BlockSpec(memory_space=pltpu.SMEM)
PAIR_WEIGHT = pl.BlockSpec((INNER, 4 * PART), lambda step: (0, 0))
REST_WEIGHT = pl.BlockSpec((INNER, 4 * PART), lambda step: (1, 0))


def call(kernel, shapes, *operands, scratch=(), flops=0, special={}, near=(), loose=()):
    def whole(leaf):
        return pl.BlockSpec(leaf.shape, lambda step: (0,) * len(leaf.shape))

    specs = [special.get(index) or whole(leaf) for index, leaf in enumerate(operands)]
    operands = [
        leaf if index in near or special.get(index) is SCALARS else pltpu.with_memory_space_constraint(leaf, pltpu.HBM)
        for index, leaf in enumerate(operands)
    ]
    return pl.pallas_call(
        kernel,
        grid=(1,),
        out_shape=[
            leaf if index in loose else pltpu.HBM(leaf.shape, leaf.dtype) for index, leaf in enumerate(shapes)
        ],
        in_specs=specs,
        out_specs=[whole(leaf) for leaf in shapes],
        scratch_shapes=list(scratch),
        compiler_params=pltpu.CompilerParams(vmem_limit_bytes=VMEM_LIMIT),
        cost_estimate=pl.CostEstimate(flops=flops, bytes_accessed=4_000_000, transcendentals=0),
    )(*operands)


def shape(*sizes, kind=BF):
    return jax.ShapeDtypeStruct(sizes, kind)


def reduce_weights(part, kept, sent):
    pieces = lax.all_to_all(part.reshape(32, 24, 2 * PART), PLANE, 0, 0, tiled=True).reshape(8, 4, 24, 2 * PART)
    pieces, sent = lax.optimization_barrier((pieces, sent))
    both = kept + partner(sent, "c")
    beside = partner(both[1].astype(BF), "yh")
    (piece,) = call(middle_kernel, [shape(16, 3, INNER)], pieces, near=(0,), loose=(0,))
    piece = lax.all_to_all(piece, Z, 0, 0, tiled=True)
    piece = jnp.sum(piece.astype(F32), 0)
    full = lax.all_to_all(jnp.broadcast_to(piece[None], (8, 3, INNER)), SLIDE, 0, 0, tiled=True)
    value_share, out_share = call(
        last_kernel, [shape(12, INNER, kind=F32), shape(6, D, kind=F32)], full, near=(0,), flops=2_500_000_000
    )
    mixed = (both[0, 0] + beside[0].astype(F32)).astype(BF)
    grad_tokens = (both[0, 1] + beside[1].astype(F32)).astype(BF)
    return mixed, grad_tokens, value_share, out_share


def one_hot(source, size):
    return (jnp.arange(size, dtype=jnp.int32)[:, None] == source[None, :]).astype(BF)


def on_device(tokens, lengths, w_query, w_key, w_value, w_out, grad_out):
    length = lengths[0]
    core, yh = lax.axis_index("c"), lax.axis_index("yh")
    zh, zl = lax.axis_index("zh"), lax.axis_index("zl")
    block = ((zh * 4 + zl) * 2 + yh) * 2 + core
    turn = (yh * 2 + core) * 2

    (mine,) = call(first_kernel, [shape(16, 3, D)], w_key, w_value, w_query, w_out, loose=(0,))
    tokens, grad_out, mine = lax.optimization_barrier((tokens, grad_out, mine))
    own = jnp.concatenate([tokens[0], grad_out[0]], 0)
    other = partner(own, "yh")
    rows = lax.all_to_all(mine, Z, 0, 0, tiled=True)
    wide = jnp.arange(D, dtype=jnp.int32)
    own, rows, length, turn, block, zl, wide = lax.optimization_barrier((own, rows, length, turn, block, zl, wide))
    (chunks,) = call(
        chunk_kernel, [shape(8, 4, 24, 4 * PART)], rows, scratch=[pltpu.VMEM((48, D), F32)], near=(0,), loose=(0,)
    )
    weights = lax.all_to_all(chunks.reshape(32, 24, 4 * PART), PLANE, 0, 0, tiled=True).reshape(D, 4 * PART)

    both = jnp.concatenate([own, other], 0)
    both = jnp.stack([both, partner(both, "c")]).reshape(2, 2, 2, TOK, D)
    inputs = both[:, :, 0].transpose(1, 0, 2, 3).reshape(QUAD, D)
    upstream_rows = both[:, :, 1].transpose(1, 0, 2, 3).reshape(QUAD, D)

    row = jnp.arange(QUAD, dtype=jnp.int32)
    which = (row >> 3) & 3
    within = ((row & 7) << 4) + (reversed4(row >> 5) ^ turn)
    order = one_hot(which * TOK + within, QUAD).T
    valid = ((block ^ (row >> 7)) * TOK + (row & 127) < length).astype(F32)[:, None]

    column = wide
    high, spot, left = column // INNER, column % INNER // 24, column % 24
    columns = one_hot(((high * 8 + left // 3) * 4 + (spot & 3)) * 12 + (spot >> 2) * 3 + left % 3, D)
    column = jnp.arange(HALF, dtype=jnp.int32)
    spot, left = column // 24, column % 24
    inner = (left % 12 // 3 * 4 + (spot & 3)) * 6 + (spot >> 2) * 3 + left % 3
    pick = one_hot(left // 12 * PART + inner, HALF)

    def key_position(member, size):
        return ((member ^ which[:size]) * TOK) + within[:size]

    base = ((row[:TOK] & 7) << 4) + (reversed4(row[:TOK] >> 3) ^ turn)
    pair_base = ((row[:TOK] & 7) << 4) + (reversed4(row[:TOK] >> 4) ^ turn)
    near_position = [(block ^ m) * TOK + base for m in range(4)]
    near_position += [((block ^ (p * 2)) ^ ((row[:TOK] >> 3) & 1)) * TOK + pair_base for p in range(2)]
    near_position = jnp.stack(near_position + near_position[:2])
    parts = [key_position(block, TOK)]
    start = (zl >> 1) * 2
    for index in range(2):
        parts.append(key_position(((zh * 4 + start + index) * 2 + yh) * 2 + core, 64))
    for index in range(4):
        parts.append(key_position(((zh * 4 + index) * 2 + yh) * 2 + core, 32))
    far_position = jnp.broadcast_to(jnp.concatenate(parts)[None], (8, FAR))
    position = jnp.concatenate([near_position, far_position], 1)

    tokens_rows = dot(order, dot(inputs, columns).astype(BF)).astype(BF)
    (
        upstream_rows, order, valid, columns, pick, position, tokens_rows,
    ) = lax.optimization_barrier(
        (upstream_rows, order, valid, columns, pick, position, tokens_rows)
    )

    (sent,) = call(
        sent_kernel,
        [shape(4, 64, 2 * PART)],
        tokens_rows, tokens_rows, weights,
        special={
            0: pl.BlockSpec((64, D), lambda step: (0, 0)),
            1: pl.BlockSpec((64, D), lambda step: (QUAD // 128, 0)),
            2: PAIR_WEIGHT,
        },
        near=(0, 1, 2),
        loose=(0,),
        flops=200_000_000,
    )
    around = lax.all_to_all(sent, "zl", 0, 0, tiled=True)
    query_rows, key_rows, out_weight = call(
        query_kernel,
        (shape(STORED, 2 * PART), shape(STORED, 2 * PART), shape(PART, D)),
        tokens_rows, upstream_rows, valid, order, pick, weights, weights,
        special={5: PAIR_WEIGHT, 6: REST_WEIGHT},
        loose=(0, 1),
        flops=3_000_000_000,
    )

    both, near_grads, around = call(
        attention_kernel,
        (shape(QUAD, 2 * PART), shape(QUAD, 2 * PART, kind=F32), shape(4, 64, 2 * PART)),
        lengths, query_rows, key_rows, around, position,
        scratch=[
            pltpu.VMEM((FAR, 2 * PART), BF), pltpu.VMEM((2 * TOK, 2 * PART), F32), pltpu.VMEM((4, 64, 2 * PART), F32),
            pltpu.VMEM((QUAD, PART), F32), pltpu.VMEM((QUAD, PART), F32),
        ],
        special={0: SCALARS},
        near=(1, 2, 3),
        loose=(2,),
        flops=3_000_000_000,
    )

    around = lax.all_to_all(around, "zl", 0, 0, tiled=True)
    attended, out_part = call(
        finish_kernel,
        (shape(QUAD, PART), shape(INNER, 2 * PART)),
        both, valid, order, pick, upstream_rows,
        flops=3_000_000_000,
    )
    (part,) = call(
        value_kernel,
        [shape(D, 2 * PART)],
        near_grads, around, tokens_rows, out_part,
        near=(1,),
        loose=(0,),
        flops=200_000_000,
    )
    kept, sent = call(
        tokens_kernel,
        (shape(2, 2, TOK, D, kind=F32), shape(2, 2, TOK, D, kind=F32)),
        attended, out_weight, both, order, near_grads, around, columns, weights, weights,
        special={7: PAIR_WEIGHT, 8: REST_WEIGHT},
        flops=3_000_000_000,
    )
    mixed, grad_tokens, value_share, out_share = reduce_weights(part, kept, sent)
    return mixed[None], grad_tokens[None], value_share, out_share


def solution(mesh):
    fine = Mesh(mesh.devices.reshape(2, 4, 4, 4, 2, 2), ("yl", "x", "zh", "zl", "yh", "c"))
    seq = ("zh", "zl", "yh", "c")
    rows = P(seq, None)
    whole = P(SLIDE, seq, None)
    return jax.shard_map(
        on_device,
        mesh=fine,
        in_specs=(whole, P(SLIDE), rows, rows, rows, rows, whole),
        out_specs=(whole, whole, rows, rows),
        check_vma=False,
    )
```

```python
import jax
import jax.numpy as jnp
from jax import lax
from jax.experimental import pallas as pl
from jax.experimental.pallas import tpu as pltpu
from jax.sharding import Mesh, PartitionSpec as P

D = 768
INNER = 384
TOK = 128
QUAD = 4 * TOK
DIM = 48
LOCAL_HEADS = 2
PART = LOCAL_HEADS * DIM
HALF = INNER // 2
STORED = QUAD + 3 * TOK
FAR = 3 * TOK
BF = jnp.bfloat16
F32 = jnp.float32
SLIDE = ("yl", "x")
Z = ("zh", "zl")
PLANE = ("yl", "x", "yh", "c")
VMEM_LIMIT = 24 * 1024 * 1024

SPLIT_TO_MIXED = [m * 128 + g * 8 for g in range(16) for m in range(4)]
MIXED_TO_SPLIT = [g * 32 + m * 8 for m in range(4) for g in range(16)]
PAIR_TO_MIXED = [(m >> 1) * 128 + g * 16 + (m & 1) * 8 for g in range(8) for m in range(4)]
MIXED_TO_PAIR = [g * 32 + (p * 2 + c) * 8 for p in range(2) for g in range(8) for c in range(2)]


def dot(a, b):
    return jnp.dot(a, b, preferred_element_type=F32)


def dot_nt(a, b):
    return lax.dot_general(a, b, (((1,), (1,)), ((), ())), preferred_element_type=F32)


def dot_tn(a, b):
    return lax.dot_general(a, b, (((0,), (0,)), ((), ())), preferred_element_type=F32)


def partner(value, axis):
    return lax.ppermute(value, axis, [(0, 1), (1, 0)])


def reversed4(value):
    return ((value & 1) << 3) | ((value & 2) << 1) | ((value & 4) >> 1) | ((value & 8) >> 3)


def regroup(rows, starts):
    return jnp.concatenate([rows[start : start + 8] for start in starts], 0)


def swap_rows(rows):
    lane = lax.broadcasted_iota(jnp.int32, rows.shape, 1)
    odd = (lane >= DIM) & (lane < 2 * DIM) | (lane >= 3 * DIM)
    moved = jnp.concatenate([rows[QUAD // 2 :], rows[: QUAD // 2]], 0)
    return jnp.where(odd, moved, rows)


def first_kernel(key_ref, value_ref, query_ref, out_weight_ref, out_ref):
    yl, x = lax.axis_index("yl"), lax.axis_index("x")
    query, key, value = (ref[...].astype(F32) for ref in (query_ref, key_ref, value_ref))
    out_weight = out_weight_ref[...].astype(F32)
    left = jnp.where(yl == 0, key, query)
    mine = None
    for index in range(4):
        rows = slice(3 * index, 3 * index + 3)
        out_rows = slice((index & 1) * 3, (index & 1) * 3 + 3)
        side = slice((index >> 1) * INNER, (index >> 1) * INNER + INNER)
        right = jnp.where(yl == 0, value[rows], out_weight[out_rows, side])
        part = jnp.concatenate([left[rows], right], 1)
        mine = part if mine is None else jnp.where(x == index, part, mine)
    out_ref[...] = jnp.broadcast_to(mine.astype(BF)[None], out_ref.shape)


def chunk_kernel(pieces_ref, out_ref, joined):
    yl = lax.axis_index("yl")
    for index in range(16):
        joined[3 * index : 3 * index + 3, :] = pieces_ref[index].astype(F32)
    rows = joined[...]
    for member in range(4):
        lanes = slice(member * PART, (member + 1) * PART)
        other = rows[member * 12 : (member + 1) * 12, INNER:]
        other = jnp.concatenate([other[:, q * PART : (q + 1) * PART] for q in range(4)], 0)
        right = jnp.where(yl == 0, rows[:, INNER:][:, lanes], other)
        chunk = jnp.concatenate([rows[:, lanes], right], 1)
        chunk = jnp.concatenate([chunk[:24], chunk[24:]], 1).astype(BF)
        for place in range(8):
            out_ref[place, member] = chunk


def project(rows, weight, lanes):
    low, high = slice(lanes.start, lanes.stop), slice(2 * PART + lanes.start, 2 * PART + lanes.stop)
    return dot(rows[:, :INNER], weight[:, low]) + dot(rows[:, INNER:], weight[:, high])


def store(out_ref, lanes, rows):
    out_ref[:QUAD, lanes] = regroup(rows, MIXED_TO_SPLIT).astype(BF)
    out_ref[QUAD : QUAD + 2 * TOK, lanes] = regroup(rows, MIXED_TO_PAIR).astype(BF)
    out_ref[QUAD + 2 * TOK :, lanes] = rows[:TOK].astype(BF)


def sent_kernel(even_ref, odd_ref, weight_ref, out_ref):
    weight = weight_ref[...]
    even, odd = (project(ref[...], weight, slice(0, 2 * PART)) for ref in (even_ref, odd_ref))
    lane = lax.broadcasted_iota(jnp.int32, even.shape, 1)
    rows = jnp.where((lane >= DIM) & (lane < 2 * DIM) | (lane >= 3 * DIM), odd, even)
    rows = jnp.concatenate([rows[:32], rows[32:]], 1).astype(BF)
    for member in range(4):
        out_ref[member] = rows


def query_kernel(
    tokens_ref, grad_out_ref, valid_ref, order_ref, pick_ref, pair_ref, rest_ref, rows_ref, key_rows_ref, out_ref
):
    lanes = slice(0, 2 * PART)
    store(key_rows_ref, lanes, swap_rows(project(tokens_ref[...], pair_ref[...], lanes)))
    rest = rest_ref[...]
    query = swap_rows(project(tokens_ref[...], rest, slice(0, PART)))
    blocks = []
    for side in range(2):
        for lanes in (slice(PART, 2 * PART), slice(3 * PART, 4 * PART)):
            block = dot(pick_ref[...], rest[side * HALF : (side + 1) * HALF, lanes])
            blocks += [block[:PART], block[PART:]]
    out_weight = jnp.concatenate(blocks, 1).astype(BF)
    out_ref[...] = out_weight
    upstream = dot_nt(grad_out_ref[...], out_weight)
    upstream = jnp.where(valid_ref[...] > 0, upstream, 0.0).astype(BF)
    upstream = swap_rows(dot(order_ref[...], upstream))
    store(rows_ref, slice(0, 2 * PART), jnp.concatenate([query, upstream], 1))


def attention_kernel(
    length_ref, query_rows_ref, key_rows_ref, around_ref, position_ref,
    out_ref, near_ref, around_out_ref, far_rows, far_ref, wide, attended, grad_query,
):
    split, pair, near = slice(0, QUAD), slice(QUAD, QUAD + 2 * TOK), slice(QUAD + 2 * TOK, STORED)
    query_split_ref, query_pair_ref, query_ref = (query_rows_ref.at[rows] for rows in (split, pair, near))
    split_ref, pair_ref, rows_ref = (key_rows_ref.at[rows] for rows in (split, pair, near))
    scale = DIM ** -0.5
    length, start = length_ref[0], (lax.axis_index("zl") >> 1) * 2
    far_rows[:TOK, :] = rows_ref[...]
    beside = around_ref[pl.ds(start, 2)]
    for index in range(4):
        half = slice((index & 1) * 2 * PART, (index & 1) * 2 * PART + 2 * PART)
        far_rows[TOK + 32 * index : TOK + 32 * index + 32, :] = beside[index >> 1, :, half]
        far_rows[2 * TOK + 32 * index : 2 * TOK + 32 * index + 32, :] = around_ref[index, :, : 2 * PART]
    place = lax.broadcasted_iota(jnp.int32, (TOK, FAR), 0)
    lane = lax.broadcasted_iota(jnp.int32, (TOK, FAR), 1)
    used = jnp.where(lane < TOK, TOK, jnp.where(lane < 2 * TOK, TOK // 2, TOK // 4))
    limit = jnp.where(place < used, length, -1)
    heads = range(LOCAL_HEADS)
    lanes = [slice(h * DIM, (h + 1) * DIM) for h in heads]
    value_lanes = [slice(PART + h * DIM, PART + (h + 1) * DIM) for h in heads]
    blocks = [slice(m * TOK, (m + 1) * TOK) for m in range(4)]
    pairs = blocks[:2]

    def grow(low, high, combine):
        size = low.shape[0]
        return jnp.concatenate([combine(high[:size], low), high[size:]], 0)

    scores, grads = [], []
    for h in heads:
        def masked(query, keys, position):
            position = position ^ h
            return jnp.where(position < length, dot_nt(query, keys) * scale, jnp.float32(-1e9))

        s0 = [masked(query_split_ref[b, lanes[h]], split_ref[b, lanes[h]], position_ref[m : m + 1, :TOK]) for m, b in enumerate(blocks)]
        s1 = [masked(query_pair_ref[b, lanes[h]], pair_ref[b, lanes[h]], position_ref[4 + p : 5 + p, :TOK]) for p, b in enumerate(pairs)]
        s2 = dot_nt(query_ref[:, lanes[h]], far_rows[:, lanes[h]]) * scale
        position = jnp.broadcast_to(position_ref[:1, TOK:] ^ h, s2.shape)
        s2 = jnp.where(position < limit, s2, jnp.float32(-1e9))
        scores.append(
            [regroup(jnp.concatenate(s0, 0), SPLIT_TO_MIXED), regroup(jnp.concatenate(s1, 0), PAIR_TO_MIXED), s2]
        )
    for h in heads:
        g0 = [dot_nt(query_split_ref[b, value_lanes[h]], split_ref[b, value_lanes[h]]) for b in blocks]
        g1 = [dot_nt(query_pair_ref[b, value_lanes[h]], pair_ref[b, value_lanes[h]]) for b in pairs]
        g2 = dot_nt(query_ref[:, value_lanes[h]], far_rows[:, value_lanes[h]])
        grads.append(
            [regroup(jnp.concatenate(g0, 0), SPLIT_TO_MIXED), regroup(jnp.concatenate(g1, 0), PAIR_TO_MIXED), g2]
        )

    weights, steps = [], []
    for h in heads:
        def rows_of(values, reduce, combine):
            total = combine(combine(values[2][:, :TOK], values[2][:, TOK : 2 * TOK]), values[2][:, 2 * TOK :])
            total = grow(grow(total, values[1], combine), values[0], combine)
            return reduce(total, axis=1, keepdims=True)

        top = rows_of(scores[h], jnp.max, jnp.maximum)
        expo = [jnp.exp(s - top[: s.shape[0]]) for s in scores[h]]
        factor = 1.0 / rows_of(expo, jnp.sum, jnp.add)
        probs = [e * factor[: e.shape[0]] for e in expo]
        delta = rows_of([p * g for p, g in zip(probs, grads[h])], jnp.sum, jnp.add)
        moved = [p * (g - delta[: p.shape[0]]) for p, g in zip(probs, grads[h])]
        for values, store in ((probs, weights), (moved, steps)):
            store.append(
                [
                    regroup(values[0], MIXED_TO_SPLIT).astype(BF),
                    regroup(values[1], MIXED_TO_PAIR).astype(BF),
                    values[2].astype(BF),
                ]
            )

    for h in heads:
        for target, left, source, factor in (
            (attended, weights[h], value_lanes[h], None), (grad_query, steps[h], lanes[h], scale)
        ):
            r0 = jnp.concatenate([dot(left[0][b], split_ref[b, source]) for b in blocks], 0)
            r1 = jnp.concatenate([dot(left[1][b], pair_ref[b, source]) for b in pairs], 0)
            r2 = dot(left[2], far_rows[:, source])
            rows = grow(r2, regroup(r1, PAIR_TO_MIXED), jnp.add)
            rows = grow(rows, regroup(r0, SPLIT_TO_MIXED), jnp.add)
            target[:, lanes[h]] = rows if factor is None else rows * factor
        for left, right, target, factor in (
            (steps[h], (query_split_ref, query_pair_ref, query_ref), lanes[h], scale),
            (weights[h], (query_split_ref, query_pair_ref, query_ref), value_lanes[h], None),
        ):
            r0 = jnp.concatenate([dot_tn(left[0][b], right[0][b, target]) for b in blocks], 0)
            r1 = jnp.concatenate([dot_tn(left[1][b], right[1][b, target]) for b in pairs], 0)
            r2 = dot_tn(left[2], right[2][:, target])
            rows = grow(r2[:TOK], regroup(r1, PAIR_TO_MIXED), jnp.add)
            rows = grow(rows, regroup(r0, SPLIT_TO_MIXED), jnp.add)
            near_ref[:, target] = rows if factor is None else rows * factor
            far_ref[:, target] = r2[TOK:] if factor is None else r2[TOK:] * factor

    wide[:, :, : 2 * PART] = far_ref[TOK:, :].reshape(4, 32, 2 * PART)
    wide[:, :, 2 * PART :] = jnp.zeros((4, 32, 2 * PART), F32)
    wide[pl.ds(start, 2)] += jnp.stack(
        [jnp.concatenate([far_ref[r : r + 32, :], far_ref[r + 32 : r + 64, :]], 1) for r in (0, 64)]
    )
    around_out_ref[...] = wide[...].astype(BF)
    rows = jnp.concatenate([attended[...], grad_query[...]], 1)
    out_ref[...] = swap_rows(rows).astype(BF)


def finish_kernel(
    attended_ref, valid_ref, order_ref, pick_ref, grad_out_ref, rows_ref, part_ref
):
    rows = jnp.where(valid_ref[...] > 0, dot_tn(order_ref[...], attended_ref[:, :PART]), 0.0).astype(BF)
    rows_ref[...] = rows
    part = dot_tn(rows, grad_out_ref[...]).astype(BF)
    for side in range(2):
        for high in range(2):
            start = side * INNER + high * 2 * PART
            stacked = jnp.concatenate([part[:, start : start + PART], part[:, start + PART : start + 2 * PART]], 0)
            part_ref[side * HALF : (side + 1) * HALF, high * PART : (high + 1) * PART] = dot_tn(
                pick_ref[...], stacked
            ).astype(BF)


def key_value_grads(near_ref, around_ref):
    rows = near_ref[...]
    first = jnp.sum(around_ref[...].astype(F32), 0)
    first = jnp.concatenate([first[:, : 2 * PART], first[:, 2 * PART :]], 0)
    rows = jnp.concatenate([rows[:64] + first, rows[64:]], 0)
    return swap_rows(rows).astype(BF)


def value_kernel(near_ref, around_ref, tokens_ref, out_part_ref, part_ref):
    rows = key_value_grads(near_ref, around_ref)
    part = dot_tn(rows[:, PART:], tokens_ref[...])
    part_ref[:INNER, :PART] = part[:, :INNER].T.astype(BF)
    part_ref[:INNER, PART:] = part[:, INNER:].T.astype(BF)
    part_ref[INNER:, :] = out_part_ref[...]


def middle_kernel(pieces_ref, out_ref):
    yl = lax.axis_index("yl")
    sums = [jnp.sum(pieces_ref[:, member].astype(F32), 0) for member in range(4)]
    halves = slice(0, PART), slice(PART, 2 * PART)
    value = [jnp.concatenate([part[:, lanes] for part in sums], 1) for lanes in halves]
    other = [
        jnp.concatenate([part[rows, lanes] for lanes in halves for rows in (slice(0, 12), slice(12, 24))], 1)
        for part in sums
    ]
    rows = jnp.where(yl == 0, jnp.concatenate(value, 0), jnp.concatenate(other, 0))
    for index in range(16):
        out_ref[index] = rows[3 * index : 3 * index + 3].astype(BF)


def last_kernel(pieces_ref, value_ref, out_ref):
    for x in range(4):
        value_ref[3 * x : 3 * x + 3, :] = pieces_ref[x]
        rows, side = (x & 1) * 3, (x >> 1) * INNER
        out_ref[rows : rows + 3, side : side + INNER] = pieces_ref[4 + x]


def tokens_kernel(
    attended_ref, out_weight_ref, grad_query_ref, order_ref, near_ref, around_ref, columns_ref, pair_ref, rest_ref,
    kept_ref, sent_ref,
):
    pair = project(columns_ref[...], pair_ref[...], slice(0, 2 * PART)).astype(BF)
    query = project(columns_ref[...], rest_ref[...], slice(0, PART)).astype(BF)
    order = order_ref[...]
    grad_query = dot_tn(order, grad_query_ref[:, PART:]).astype(BF)
    grad_rows = dot_tn(order, key_value_grads(near_ref, around_ref)).astype(BF)
    mixed = dot(attended_ref[...], out_weight_ref[...])
    grads = dot_nt(grad_query, query) + dot_nt(grad_rows, pair)
    for index, rows in enumerate((mixed, grads)):
        for side in range(2):
            start = side * 2 * TOK
            kept_ref[side, index] = rows[start : start + TOK]
            sent_ref[side, index] = rows[start + TOK : start + 2 * TOK]


SCALARS = pl.BlockSpec(memory_space=pltpu.SMEM)
PAIR_WEIGHT = pl.BlockSpec((INNER, 4 * PART), lambda step: (0, 0))
REST_WEIGHT = pl.BlockSpec((INNER, 4 * PART), lambda step: (1, 0))


def call(kernel, shapes, *operands, scratch=(), flops=0, special={}, near=(), loose=()):
    def whole(leaf):
        return pl.BlockSpec(leaf.shape, lambda step: (0,) * len(leaf.shape))

    specs = [special.get(index) or whole(leaf) for index, leaf in enumerate(operands)]
    operands = [
        leaf if index in near or special.get(index) is SCALARS else pltpu.with_memory_space_constraint(leaf, pltpu.HBM)
        for index, leaf in enumerate(operands)
    ]
    return pl.pallas_call(
        kernel,
        grid=(1,),
        out_shape=[
            leaf if index in loose else pltpu.HBM(leaf.shape, leaf.dtype) for index, leaf in enumerate(shapes)
        ],
        in_specs=specs,
        out_specs=[whole(leaf) for leaf in shapes],
        scratch_shapes=list(scratch),
        compiler_params=pltpu.CompilerParams(vmem_limit_bytes=VMEM_LIMIT),
        cost_estimate=pl.CostEstimate(flops=flops, bytes_accessed=4_000_000, transcendentals=0),
    )(*operands)


def shape(*sizes, kind=BF):
    return jax.ShapeDtypeStruct(sizes, kind)


def reduce_weights(part, kept, sent):
    pieces = lax.all_to_all(part.reshape(32, 24, 2 * PART), PLANE, 0, 0, tiled=True).reshape(8, 4, 24, 2 * PART)
    pieces, sent = lax.optimization_barrier((pieces, sent))
    both = kept + partner(sent, "c")
    beside = partner(both[1].astype(BF), "yh")
    (piece,) = call(middle_kernel, [shape(16, 3, INNER)], pieces, near=(0,), loose=(0,))
    piece = lax.all_to_all(piece, Z, 0, 0, tiled=True)
    piece = jnp.sum(piece.astype(F32), 0)
    full = lax.all_to_all(jnp.broadcast_to(piece[None], (8, 3, INNER)), SLIDE, 0, 0, tiled=True)
    value_share, out_share = call(
        last_kernel, [shape(12, INNER, kind=F32), shape(6, D, kind=F32)], full, near=(0,), flops=2_500_000_000
    )
    mixed = (both[0, 0] + beside[0].astype(F32)).astype(BF)
    grad_tokens = (both[0, 1] + beside[1].astype(F32)).astype(BF)
    return mixed, grad_tokens, value_share, out_share


def one_hot(source, size):
    return (jnp.arange(size, dtype=jnp.int32)[:, None] == source[None, :]).astype(BF)


def on_device(tokens, lengths, w_query, w_key, w_value, w_out, grad_out):
    length = lengths[0]
    core, yh = lax.axis_index("c"), lax.axis_index("yh")
    zh, zl = lax.axis_index("zh"), lax.axis_index("zl")
    block = ((zh * 4 + zl) * 2 + yh) * 2 + core
    turn = (yh * 2 + core) * 2

    (mine,) = call(first_kernel, [shape(16, 3, D)], w_key, w_value, w_query, w_out, loose=(0,))
    tokens, grad_out, mine = lax.optimization_barrier((tokens, grad_out, mine))
    own = jnp.concatenate([tokens[0], grad_out[0]], 0)
    other = partner(own, "yh")
    rows = lax.all_to_all(mine, Z, 0, 0, tiled=True)
    wide = jnp.arange(D, dtype=jnp.int32)
    own, rows, length, turn, block, zl, wide = lax.optimization_barrier((own, rows, length, turn, block, zl, wide))
    (chunks,) = call(
        chunk_kernel, [shape(8, 4, 24, 4 * PART)], rows, scratch=[pltpu.VMEM((48, D), F32)], near=(0,), loose=(0,)
    )
    weights = lax.all_to_all(chunks.reshape(32, 24, 4 * PART), PLANE, 0, 0, tiled=True).reshape(D, 4 * PART)

    both = jnp.concatenate([own, other], 0)
    both = jnp.stack([both, partner(both, "c")]).reshape(2, 2, 2, TOK, D)
    inputs = both[:, :, 0].transpose(1, 0, 2, 3).reshape(QUAD, D)
    upstream_rows = both[:, :, 1].transpose(1, 0, 2, 3).reshape(QUAD, D)

    row = jnp.arange(QUAD, dtype=jnp.int32)
    which = (row >> 3) & 3
    within = ((row & 7) << 4) + (reversed4(row >> 5) ^ turn)
    order = one_hot(which * TOK + within, QUAD).T
    valid = ((block ^ (row >> 7)) * TOK + (row & 127) < length).astype(F32)[:, None]

    column = wide
    high, spot, left = column // INNER, column % INNER // 24, column % 24
    columns = one_hot(((high * 8 + left // 3) * 4 + (spot & 3)) * 12 + (spot >> 2) * 3 + left % 3, D)
    column = jnp.arange(HALF, dtype=jnp.int32)
    spot, left = column // 24, column % 24
    inner = (left % 12 // 3 * 4 + (spot & 3)) * 6 + (spot >> 2) * 3 + left % 3
    pick = one_hot(left // 12 * PART + inner, HALF)

    def key_position(member, size):
        return ((member ^ which[:size]) * TOK) + within[:size]

    base = ((row[:TOK] & 7) << 4) + (reversed4(row[:TOK] >> 3) ^ turn)
    pair_base = ((row[:TOK] & 7) << 4) + (reversed4(row[:TOK] >> 4) ^ turn)
    near_position = [(block ^ m) * TOK + base for m in range(4)]
    near_position += [((block ^ (p * 2)) ^ ((row[:TOK] >> 3) & 1)) * TOK + pair_base for p in range(2)]
    near_position = jnp.stack(near_position + near_position[:2])
    parts = [key_position(block, TOK)]
    start = (zl >> 1) * 2
    for index in range(2):
        parts.append(key_position(((zh * 4 + start + index) * 2 + yh) * 2 + core, 64))
    for index in range(4):
        parts.append(key_position(((zh * 4 + index) * 2 + yh) * 2 + core, 32))
    far_position = jnp.broadcast_to(jnp.concatenate(parts)[None], (8, FAR))
    position = jnp.concatenate([near_position, far_position], 1)

    tokens_rows = dot(order, dot(inputs, columns).astype(BF)).astype(BF)
    (
        upstream_rows, order, valid, columns, pick, position, tokens_rows,
    ) = lax.optimization_barrier(
        (upstream_rows, order, valid, columns, pick, position, tokens_rows)
    )

    (sent,) = call(
        sent_kernel,
        [shape(4, 32, 4 * PART)],
        tokens_rows, tokens_rows, weights,
        special={
            0: pl.BlockSpec((64, D), lambda step: (0, 0)),
            1: pl.BlockSpec((64, D), lambda step: (QUAD // 128, 0)),
            2: PAIR_WEIGHT,
        },
        near=(0, 1, 2),
        loose=(0,),
        flops=200_000_000,
    )
    around = lax.all_to_all(sent, "zl", 0, 0, tiled=True)
    query_rows, key_rows, out_weight = call(
        query_kernel,
        (shape(STORED, 2 * PART), shape(STORED, 2 * PART), shape(PART, D)),
        tokens_rows, upstream_rows, valid, order, pick, weights, weights,
        special={5: PAIR_WEIGHT, 6: REST_WEIGHT},
        loose=(0, 1),
        flops=3_000_000_000,
    )

    both, near_grads, around = call(
        attention_kernel,
        (shape(QUAD, 2 * PART), shape(QUAD, 2 * PART, kind=F32), shape(4, 32, 4 * PART)),
        lengths, query_rows, key_rows, around, position,
        scratch=[
            pltpu.VMEM((FAR, 2 * PART), BF), pltpu.VMEM((2 * TOK, 2 * PART), F32), pltpu.VMEM((4, 32, 4 * PART), F32),
            pltpu.VMEM((QUAD, PART), F32), pltpu.VMEM((QUAD, PART), F32),
        ],
        special={0: SCALARS},
        near=(1, 2, 3),
        loose=(2,),
        flops=3_000_000_000,
    )

    around = lax.all_to_all(around, "zl", 0, 0, tiled=True)
    attended, out_part = call(
        finish_kernel,
        (shape(QUAD, PART), shape(INNER, 2 * PART)),
        both, valid, order, pick, upstream_rows,
        flops=3_000_000_000,
    )
    (part,) = call(
        value_kernel,
        [shape(D, 2 * PART)],
        near_grads, around, tokens_rows, out_part,
        near=(1,),
        loose=(0,),
        flops=200_000_000,
    )
    kept, sent = call(
        tokens_kernel,
        (shape(2, 2, TOK, D, kind=F32), shape(2, 2, TOK, D, kind=F32)),
        attended, out_weight, both, order, near_grads, around, columns, weights, weights,
        special={7: PAIR_WEIGHT, 8: REST_WEIGHT},
        flops=3_000_000_000,
    )
    mixed, grad_tokens, value_share, out_share = reduce_weights(part, kept, sent)
    return mixed[None], grad_tokens[None], value_share, out_share


def solution(mesh):
    fine = Mesh(mesh.devices.reshape(2, 4, 4, 4, 2, 2), ("yl", "x", "zh", "zl", "yh", "c"))
    seq = ("zh", "zl", "yh", "c")
    rows = P(seq, None)
    whole = P(SLIDE, seq, None)
    return jax.shard_map(
        on_device,
        mesh=fine,
        in_specs=(whole, P(SLIDE), rows, rows, rows, rows, whole),
        out_specs=(whole, whole, rows, rows),
        check_vma=False,
    )
```
